32 devices in a mesh: seq: 8 (over y, x, core), batch: 4 (over z).
Axes of the slice: x: 2, y: 2, z: 4, core: 2. Of those that a mesh axis runs over, the one named last changes fastest.
Arguments:
- tokens: bfloat16 [4, 2048, 2048], P('batch', 'seq'), may hold values from -6 to 6
- out_cotangent: bfloat16 [4, 2048, 2048], P('batch', 'seq'), may hold values from -6 to 6
- group_ids: int32 [4, 2048], P('batch', 'seq'), may hold values from 0 to 15, as said below
- attn_gain: bfloat16 [2048], P(('seq', 'batch')), may hold values from 0.5 to 1.5
- query_weight: bfloat16 [2048, 2048], P(('seq', 'batch')), may hold values from -0.125 to 0.125
- key_weight: bfloat16 [2048, 2048], P(('seq', 'batch')), may hold values from -0.125 to 0.125
- value_weight: bfloat16 [2048, 2048], P(('seq', 'batch')), may hold values from -0.125 to 0.125
- out_weight: bfloat16 [2048, 2048], P(('seq', 'batch')), may hold values from -0.5 to 0.5
- ffn_gain: bfloat16 [2048], P(('seq', 'batch')), may hold values from 0.5 to 1.5
- gate_weight: bfloat16 [2048, 5632], P(('seq', 'batch')), may hold values from -0.125 to 0.125
- up_weight: bfloat16 [2048, 5632], P(('seq', 'batch')), may hold values from -0.125 to 0.125
- down_weight: bfloat16 [5632, 2048], P(('seq', 'batch')), may hold values from -0.078125 to 0.078125
Outputs:
- block_out: bfloat16 [4, 2048, 2048], P('batch', 'seq')
- tokens_grad: float32 [4, 2048, 2048], P('batch', 'seq')
- attn_gain_grad: float32 [2048], P(('seq', 'batch'))
- query_grad: float32 [2048, 2048], P(('seq', 'batch'))
- key_grad: float32 [2048, 2048], P(('seq', 'batch'))
- value_grad: float32 [2048, 2048], P(('seq', 'batch'))
- out_grad: float32 [2048, 2048], P(('seq', 'batch'))
- ffn_gain_grad: float32 [2048], P(('seq', 'batch'))
- gate_grad: float32 [2048, 5632], P(('seq', 'batch'))
- up_grad: float32 [2048, 5632], P(('seq', 'batch'))
- down_grad: float32 [5632, 2048], P(('seq', 'batch'))
The draws below stay inside these ranges and needn't reach their ends.
Inputs may be any that keep to these rules, and one draw needn't show every extreme that they name: `group_ids`: sequence s (its index along the first dimension) carries only the ids s * 4 to s * 4 + 3, and each of them.
All inputs are finite; a program needn't handle non-finite values.
Results may differ from the reference program's by a relative error of at most 0.015.
Values may be sent and summed in bfloat16 or wider, within the bound.
No kernel may reach another device: no remote copies, remote signals or barrier semaphores. Data moves between devices by JAX's collectives and lax.ppermute only.
A program may use at most 704 MiB of HBM per device.

```python
import jax
import jax.numpy as jnp
from jax import lax

D = 2048
FF = 5632
HEADS = 16
HEAD = 128
WINDOW = 64
GPS = 4
SEQS = 4
LEN = 2048
GROUPS = 16


def draw_group_ids(key, part):
    key = jax.random.fold_in(key, 7)
    place = jnp.arange(LEN, dtype=jnp.int32)
    band = GPS * place * place // (LEN * LEN)
    jitter = jax.random.randint(key, (SEQS, LEN), -1, 2, dtype=jnp.int32)
    local_ids = jnp.clip(band[None, :] + jitter, 0, GPS - 1)
    return local_ids + GPS * jnp.arange(SEQS, dtype=jnp.int32)[:, None]


def block_levels(stream_key, extent, shards, smallest, high):
    level = 1.0
    for dim, blocks in shards:
        draws = jax.random.uniform(jax.random.fold_in(jax.random.fold_in(stream_key, 6), dim), (blocks,), jnp.float32, smallest / len(shards), high / len(shards))
        level = level * jnp.repeat(jnp.exp(draws), extent[dim] // blocks).reshape((-1,) + (1,) * (len(extent) - 1 - dim))
    return level


def centred(rng, shape, spread, reach, split=(), kind=jnp.bfloat16):
    drawn = jax.random.normal(rng, shape, jnp.float32) * spread
    if len(split) > 0:
        drawn = block_levels(rng, shape, split, -0.22, 0.18) * drawn
    return jnp.clip(drawn, min=-reach, max=reach).astype(kind)


def setup_inputs(seed: int = 0) -> dict:
    splits = jax.random.split(jax.random.key(seed), 13)
    return {
        "tokens": centred(splits[0], (SEQS, LEN, D), 1.0, 6.0, ((0, 4), (1, 8))),
        "out_cotangent": centred(splits[1], (SEQS, LEN, D), 1.0, 6.0, ((0, 4), (1, 8))),
        "group_ids": draw_group_ids(jax.random.fold_in(splits[12], 71), 0),
        "attn_gain": jnp.clip(1.0 + 0.1 * jax.random.normal(splits[3], (D,), jnp.float32), 0.5, 1.5).astype(jnp.bfloat16),
        "query_weight": centred(splits[4], (D, D), D ** -0.5, 0.125, ((0, 32),)),
        "key_weight": centred(splits[5], (D, D), D ** -0.5, 0.125, ((0, 32),)),
        "value_weight": centred(splits[6], (D, D), D ** -0.5, 0.125, ((0, 32),)),
        "out_weight": centred(splits[7], (D, D), (D // 16) ** -0.5, 0.5, ((0, 32),)),
        "ffn_gain": jnp.clip(1.0 + 0.1 * jax.random.normal(splits[8], (D,), jnp.float32), 0.5, 1.5).astype(jnp.bfloat16),
        "gate_weight": centred(splits[9], (D, FF), D ** -0.5, 0.125, ((0, 32),)),
        "up_weight": centred(splits[10], (D, FF), D ** -0.5, 0.125, ((0, 32),)),
        "down_weight": centred(splits[11], (FF, D), FF ** -0.5, 0.078125, ((0, 32),)),
    }


EPS = 1e-05

@jax.custom_vjp
def low(v):
    return lax.optimization_barrier(v.astype(jnp.bfloat16)).astype(jnp.float32)

@jax.custom_vjp
def low_back(v):
    return v

def low_keep(v):
    return (low(v), None)

def low_pass(kept, grad):
    return (grad,)

def back_keep(v):
    return (v, None)

def back_low(kept, grad):
    return (low(grad),)
low.defvjp(low_keep, low_pass)
low_back.defvjp(back_keep, back_low)

def rms_scale(values, gain):
    return values * lax.rsqrt(lax.optimization_barrier(jnp.mean(values * values, axis=-1, keepdims=True)) + EPS) * gain

def window_attention(queries, keys_in, values_in):
    highest = lax.Precision.HIGHEST
    length = queries.shape[0]
    block_rows = 512 if length % 512 == 0 else length
    query_heads = queries.reshape(length, HEADS, HEAD)
    key_heads = jnp.pad(keys_in.reshape(length, HEADS, HEAD), ((WINDOW, 0), (0, 0), (0, 0)))
    value_heads = jnp.pad(values_in.reshape(length, HEADS, HEAD), ((WINDOW, 0), (0, 0), (0, 0)))
    factor = HEAD ** (-0.5)

    def one_block(start):
        query_block = lax.dynamic_slice_in_dim(query_heads, start, block_rows, 0)
        key_block = lax.dynamic_slice_in_dim(key_heads, start, block_rows + WINDOW, 0)
        value_block = lax.dynamic_slice_in_dim(value_heads, start, block_rows + WINDOW, 0)
        scores = low_back(jnp.einsum('qhe,khe->hqk', query_block, key_block, precision=highest) * factor)
        query_place = start + jnp.arange(block_rows, dtype=jnp.int32)
        key_place = start - WINDOW + jnp.arange(block_rows + WINDOW, dtype=jnp.int32)
        distance = query_place[:, None] - key_place[None, :]
        allowed = (distance >= 0) & (distance < WINDOW) & (key_place[None, :] >= 0)
        scores = jnp.where(allowed[None], scores, -1e+30)
        expo = jnp.exp(scores - lax.optimization_barrier(jnp.max(scores, axis=-1, keepdims=True)))
        probs = low(expo / lax.optimization_barrier(jnp.sum(expo, axis=-1, keepdims=True)))
        mixed = jnp.einsum('hqk,khe->qhe', probs, value_block, precision=highest)
        return mixed.reshape(block_rows, HEADS * HEAD)
    starts = jnp.arange(length // block_rows, dtype=jnp.int32) * block_rows
    return lax.map(jax.checkpoint(one_block), starts).reshape(length, HEADS * HEAD)

def layer(seq_rows, attn_gain, query_weight, key_weight, value_weight, out_weight, ffn_gain, gate_weight, up_weight, down_weight):
    highest = lax.Precision.HIGHEST
    normed = low(rms_scale(seq_rows, attn_gain))
    queries = low_back(low(jnp.dot(normed, query_weight, precision=highest)))
    keys_now = low_back(low(jnp.dot(normed, key_weight, precision=highest)))
    values_now = low_back(low(jnp.dot(normed, value_weight, precision=highest)))
    mixed = low_back(low(window_attention(queries, keys_now, values_now)))
    resid = seq_rows + low_back(jnp.dot(mixed, out_weight, precision=highest))
    normed_ffn = low(rms_scale(resid, ffn_gain))
    gate = low_back(jnp.dot(normed_ffn, gate_weight, precision=highest))
    upward = low_back(jnp.dot(normed_ffn, up_weight, precision=highest))
    hidden = low(jax.nn.silu(gate) * upward)
    return resid + low_back(jnp.dot(hidden, down_weight, precision=highest))

def reference(tokens, out_cotangent, group_ids, attn_gain, query_weight, key_weight, value_weight, out_weight, ffn_gain, gate_weight, up_weight, down_weight):
    params = (attn_gain.astype(jnp.float32), query_weight.astype(jnp.float32), key_weight.astype(jnp.float32), value_weight.astype(jnp.float32), out_weight.astype(jnp.float32), ffn_gain.astype(jnp.float32), gate_weight.astype(jnp.float32), up_weight.astype(jnp.float32), down_weight.astype(jnp.float32))
    onehot = (group_ids[:, :, None] == jnp.arange(GROUPS, dtype=jnp.int32)[None, None, :]).astype(jnp.float32)
    group_total = lax.optimization_barrier(jnp.sum(onehot, axis=(0, 1)))
    own_total = lax.optimization_barrier(jnp.sum(onehot * group_total, axis=-1))
    weighting = jnp.float32(LEN) / (GPS * own_total)

    def one_sequence(totals, inputs):
        seq_rows, seq_cot, seq_weight = inputs
        outcome, pullback = jax.vjp(layer, seq_rows.astype(jnp.float32), *params)
        grads = pullback(seq_cot.astype(jnp.float32) * seq_weight[:, None])
        totals = tuple((total + grad for total, grad in zip(totals, grads[1:])))
        return (totals, (outcome.astype(jnp.bfloat16), grads[0]))
    start_totals = tuple((jnp.zeros(param.shape, jnp.float32) for param in params))
    totals, (block_out, tokens_grad) = lax.scan(one_sequence, start_totals, (tokens, out_cotangent, weighting))
    return (block_out, tokens_grad, totals[0], totals[1], totals[2], totals[3], totals[4], totals[5], totals[6], totals[7], totals[8])
```

```python
import jax
import jax.numpy as jnp
from jax import lax
from jax.sharding import PartitionSpec as P

HEAD = 128
WINDOW = 64
GPS = 4
CORES = 2

EPS = 1e-05
NEGATIVE = -1e30
ROWS_DIMS = (((0,), (0,)), ((), ()))
COLS_DIMS = (((1,), (1,)), ((), ()))
BLOCK = 128
F32 = jnp.float32
LOW = jnp.bfloat16


def matmul(left, right):
    return jnp.dot(left, right, preferred_element_type=F32)


def matmul_rows(left, right):
    return lax.dot_general(left, right, ROWS_DIMS, preferred_element_type=F32)


def matmul_cols(left, right):
    return lax.dot_general(left, right, COLS_DIMS, preferred_element_type=F32)


def exchange(value, flip):
    count = lax.axis_size("seq")
    return lax.ppermute(value, "seq", [(place, place ^ flip) for place in range(count)])


def swap_core(value):
    return exchange(value, 1)


def chip_count():
    return lax.axis_size("seq") // CORES


def own_chip():
    return lax.axis_index("seq") // CORES


def own_core():
    return lax.axis_index("seq") % CORES


def chips_gather(value):
    return [value] + [exchange(value, CORES * k) for k in range(1, chip_count())]


def chips_scatter(blocks):
    return [blocks[0]] + [exchange(blocks[k], CORES * k) for k in range(1, chip_count())]


def in_order(blocks):
    chip = own_chip()
    bit = 1
    while bit < len(blocks):
        flipped = (chip & bit) > 0
        blocks = [jnp.where(flipped, blocks[i ^ bit], blocks[i]) for i in range(len(blocks))]
        bit *= 2
    return blocks


def to_chips(value):
    chip = own_chip()
    blocks = [
        lax.dynamic_index_in_dim(value, chip ^ k, axis=0, keepdims=False)
        for k in range(chip_count())
    ]
    return jnp.stack(in_order(chips_scatter(blocks)))


def to_own(values):
    rows = values.shape[:-1]
    parts = values.reshape(rows + (chip_count(), CORES, -1))
    flipped = own_core() > 0
    first, second = parts[..., 0, :], parts[..., 1, :]
    mine = jnp.where(flipped, second, first).reshape(rows + (-1,))
    other = jnp.where(flipped, first, second).reshape(rows + (-1,))
    return jnp.concatenate([mine, other], axis=-1)


def from_own(values):
    rows = values.shape[:-1]
    half = values.shape[-1] // CORES
    mine, other = values[..., :half], values[..., half:]
    flipped = own_core() > 0
    first = jnp.where(flipped, other, mine).reshape(rows + (chip_count(), 1, -1))
    second = jnp.where(flipped, mine, other).reshape(rows + (chip_count(), 1, -1))
    return jnp.concatenate([first, second], axis=-2).reshape(values.shape)


def core_rows(mine, other):
    flipped = own_core() > 0
    return jnp.concatenate(
        [jnp.where(flipped, other, mine), jnp.where(flipped, mine, other)], axis=0
    )


def core_reduce(first, second):
    flipped = own_core() > 0
    mine = jnp.where(flipped, second, first)
    other = jnp.where(flipped, first, second).astype(LOW)
    return mine + swap_core(other).astype(F32)


def batch_gather(value, axis):
    return lax.all_gather(value, "batch", axis=axis, tiled=True)


def batch_scatter(value, axis):
    return lax.psum_scatter(value, "batch", scatter_dimension=axis, tiled=True)


def to_heads(values):
    return values.reshape(values.shape[:-1] + (values.shape[-1] // HEAD, HEAD))


def blocks_with_rim(values, rim, block_rows):
    seq_count, tok_count, features = values.shape
    rim_rows = rim.shape[1]
    owned = values.reshape(seq_count, tok_count // block_rows, block_rows, features)
    before = jnp.concatenate([rim[:, None], owned[:, :-1, block_rows - rim_rows :]], axis=1)
    return jnp.concatenate([before, owned], axis=2)


def window_allowed(block_count, block_rows, rim_rows, preceded):
    query_place = jnp.arange(block_rows, dtype=jnp.int32)[:, None]
    key_place = jnp.arange(block_rows + rim_rows, dtype=jnp.int32)[None, :] - rim_rows
    distance = query_place - key_place
    inside = (distance >= 0) & (distance < rim_rows)
    block_index = jnp.arange(block_count, dtype=jnp.int32)[:, None, None]
    reach = (
        (block_index > 0)[None] | (key_place[None, None] >= 0) | preceded[:, None, None, None]
    )
    return inside[None, None] & reach


def window_scores(query_blocks, key_blocks, allowed):
    scores = jnp.einsum(
        "snqhe,snkhe->snhqk", query_blocks, key_blocks, preferred_element_type=F32
    ) * HEAD ** (-0.5)
    return jnp.where(allowed[:, :, None], scores, NEGATIVE)


def attend(query_blocks, key_blocks, value_blocks, allowed):
    scores = window_scores(query_blocks, key_blocks, allowed)
    top = jnp.max(scores, axis=-1, keepdims=True)
    expo = jnp.exp(scores - top)
    total = jnp.sum(expo, axis=-1, keepdims=True)
    probs_low = (expo / total).astype(LOW)
    mixed = jnp.einsum("snhqk,snkhe->snqhe", probs_low, value_blocks, preferred_element_type=F32)
    return (mixed, top + jnp.log(total))


def attend_back(query_blocks, key_blocks, value_blocks, allowed, log_total, d_mixed_blocks):
    probs = jnp.exp(window_scores(query_blocks, key_blocks, allowed) - log_total)
    probs_again = probs.astype(LOW)
    d_probs = jnp.einsum(
        "snqhe,snkhe->snhqk", d_mixed_blocks, value_blocks, preferred_element_type=F32
    )
    d_scores = (probs * (d_probs - jnp.sum(probs * d_probs, axis=-1, keepdims=True))).astype(LOW)
    factor = HEAD ** (-0.5)
    d_query = (
        jnp.einsum("snhqk,snkhe->snqhe", d_scores, key_blocks, preferred_element_type=F32) * factor
    )
    d_keys = (
        jnp.einsum("snhqk,snqhe->snkhe", d_scores, query_blocks, preferred_element_type=F32)
        * factor
    )
    d_values = jnp.einsum(
        "snhqk,snqhe->snkhe", probs_again, d_mixed_blocks, preferred_element_type=F32
    )
    return (d_query, d_keys, d_values)


def fold_rims(d_blocks, arrived, block_rows):
    later = jnp.concatenate([d_blocks[:, :, 1:, :WINDOW], arrived[:, :, None]], axis=2)
    padded = jnp.pad(later, ((0, 0), (0, 0), (0, 0), (block_rows - WINDOW, 0), (0, 0)))
    return d_blocks[:, :, :, WINDOW:] + padded


def norm_back(d_act, gain, normed, inverse, upstream):
    scaled = d_act * gain
    return upstream + inverse * (
        scaled - normed * jnp.mean(scaled * normed, axis=-1, keepdims=True)
    )


def rms(values):
    inverse = lax.rsqrt(jnp.mean(values * values, axis=-1, keepdims=True) + EPS)
    return inverse, values * inverse


def per_device(
    tokens,
    out_cotangent,
    group_ids,
    attn_gain,
    query_weight,
    key_weight,
    value_weight,
    out_weight,
    ffn_gain,
    gate_weight,
    up_weight,
    down_weight,
):
    tok_count, features = tokens.shape[1:]
    weight_rows, inner = gate_weight.shape
    chips = chip_count()
    chip, core = own_chip(), own_core()
    ids = lax.iota(jnp.int32, chips)
    head_width, inner_width = features // chips, inner // chips

    gains = jnp.concatenate(
        [
            jnp.broadcast_to(attn_gain[:, None], (weight_rows, HEAD // 2)),
            jnp.broadcast_to(ffn_gain[:, None], (weight_rows, HEAD // 2)),
        ],
        axis=1,
    )

    def by_chip(weight):
        return weight.reshape(weight_rows, chips, -1).transpose(1, 0, 2)

    qkv_rows = to_chips(
        jnp.concatenate(
            [by_chip(query_weight), by_chip(key_weight), by_chip(value_weight)]
            + [jnp.broadcast_to(gains, (chips,) + gains.shape)],
            axis=2,
        )
    )
    qkv_mine = batch_gather(qkv_rows, 1).reshape(features // CORES, -1)
    out_mine = batch_gather(out_weight, 0)
    inner_rows = to_chips(jnp.concatenate([by_chip(gate_weight), by_chip(up_weight)], axis=2))
    inner_mine = batch_gather(inner_rows, 1).reshape(features // CORES, -1)
    down_mine = batch_gather(down_weight, 0)

    qkv_whole = jnp.concatenate([qkv_mine, swap_core(qkv_mine)], axis=0)
    qkv_own = qkv_whole[:, : 3 * head_width]
    gain_one_own = qkv_whole[:, 3 * head_width].astype(F32)
    gain_two = from_own(qkv_whole[:, 3 * head_width + HEAD // 2].astype(F32))
    out_own = core_rows(out_mine, swap_core(out_mine))
    inner_own = jnp.concatenate([inner_mine, swap_core(inner_mine)], axis=0)
    down_own = core_rows(down_mine, swap_core(down_mine))

    group_span = GPS * lax.axis_size("batch")
    onehot = (group_ids[0, :, None] == jnp.arange(group_span, dtype=jnp.int32)[None, :]).astype(F32)
    group_total = lax.psum(jnp.sum(onehot, axis=0), "seq")
    own_total = jnp.sum(onehot * group_total, axis=-1)[:, None]
    weighting = tok_count * lax.axis_size("seq") / (GPS * own_total)
    d_final = out_cotangent[0].astype(F32) * weighting
    d_ffn = jnp.concatenate(chips_gather(d_final.astype(LOW)), axis=0)

    flat = tokens[0].astype(F32)
    inverse_one, normed_one = rms(flat)
    gathered = jnp.concatenate(chips_gather(to_own(tokens[0])), axis=0).astype(F32)
    _, normed_all = rms(gathered)
    act_one = (normed_all * gain_one_own).astype(LOW)
    qkv = matmul(act_one, qkv_own).astype(LOW).reshape(chips, tok_count, -1)
    queries, keys_low, values_low = (
        qkv[..., :head_width],
        qkv[..., head_width : 2 * head_width],
        qkv[..., 2 * head_width :],
    )
    place = chip ^ ids
    tails = swap_core(qkv[:, tok_count - WINDOW :, head_width:])
    before = jnp.where(core > 0, ids, chip ^ jnp.maximum(place - 1, 0))
    after = jnp.where(core > 0, chip ^ jnp.minimum(place + 1, chips - 1), ids)
    preceded = (core > 0) | (place > 0)
    followed = (core == 0) | (place < chips - 1)
    rims = jnp.take(tails, before, axis=0)
    key_blocks = to_heads(blocks_with_rim(keys_low, rims[..., :head_width], BLOCK))
    value_blocks = to_heads(blocks_with_rim(values_low, rims[..., head_width:], BLOCK))
    block_count = tok_count // BLOCK
    query_blocks = to_heads(queries.reshape(chips, block_count, BLOCK, head_width))
    allowed = window_allowed(block_count, BLOCK, WINDOW, preceded)
    mixed, log_total = attend(query_blocks, key_blocks, value_blocks, allowed)
    mixed_low = mixed.reshape(chips * tok_count, head_width).astype(LOW)

    def chips_sum(parts):
        parts = parts.reshape(chips, tok_count, -1)
        arrived = chips_scatter([parts[0]] + [parts[k].astype(LOW) for k in range(1, chips)])
        return sum(part.astype(F32) for part in arrived)

    resid = flat + chips_sum(matmul(mixed_low, out_own))

    inverse_two, normed_two = rms(resid)
    act_two_own = (normed_two * gain_two).astype(LOW)
    act_two = jnp.concatenate(chips_gather(to_own(act_two_own)), axis=0)
    gate_up = matmul(act_two, inner_own)
    gate, upward = gate_up[:, :inner_width], gate_up[:, inner_width:]
    sigma = jax.nn.sigmoid(gate)
    hidden = (gate * sigma * upward).astype(LOW)
    d_hidden = matmul_cols(d_ffn, down_own)
    d_gate = (d_hidden * upward * sigma * (1.0 + gate * (1.0 - sigma))).astype(LOW)
    d_up = (d_hidden * gate * sigma).astype(LOW)
    d_gate_up = jnp.concatenate([d_gate, d_up], axis=1)
    d_act_two = from_own(chips_sum(matmul_cols(d_gate_up, inner_own)))
    d_resid = norm_back(d_act_two, gain_two, normed_two, inverse_two, d_final)
    gain_two_part = to_own(jnp.sum(d_act_two * normed_two, axis=0))
    block_out = (resid + chips_sum(matmul(hidden, down_own))).astype(LOW)

    down_part = matmul_rows(hidden, d_ffn)
    down_half = inner_width // CORES
    down_sum = core_reduce(down_part[:down_half], down_part[down_half:])
    down_grad = batch_scatter(down_sum.astype(LOW), 0).astype(F32)

    def own_reduce(part):
        half = features // CORES
        summed = part[:half] + swap_core(part[half:].astype(LOW)).astype(F32)
        return batch_scatter(summed.astype(LOW).reshape(chips, half // chips, -1), 1)

    inner_grad = to_chips(own_reduce(matmul_rows(act_two, d_gate_up))).astype(F32)
    gate_grad = inner_grad[..., :inner_width].transpose(1, 0, 2).reshape(weight_rows, inner)
    up_grad = inner_grad[..., inner_width:].transpose(1, 0, 2).reshape(weight_rows, inner)

    d_attn = jnp.concatenate(chips_gather(d_resid.astype(LOW)), axis=0)
    d_mixed = matmul_cols(d_attn, out_own).astype(LOW)
    d_mixed_blocks = to_heads(d_mixed.reshape(chips, block_count, BLOCK, head_width))
    d_query, d_key_blocks, d_value_blocks = attend_back(
        query_blocks, key_blocks, value_blocks, allowed, log_total, d_mixed_blocks
    )
    d_both = jnp.stack([d_key_blocks, d_value_blocks]).reshape(
        2, chips, block_count, BLOCK + WINDOW, head_width
    )
    lent = swap_core(d_both[:, :, 0, :WINDOW].astype(LOW))
    returned = jnp.where(
        followed[None, :, None, None], jnp.take(lent, after, axis=1).astype(F32), 0.0
    )
    d_owned = fold_rims(d_both, returned, BLOCK).reshape(2, chips * tok_count, head_width)
    d_qkv = jnp.concatenate(
        [d_query.reshape(chips * tok_count, head_width), d_owned[0], d_owned[1]], axis=1
    ).astype(LOW)
    d_act_one = matmul_cols(d_qkv, qkv_own)
    gain_one_part = jnp.sum(d_act_one * normed_all, axis=0)
    tokens_grad = norm_back(
        from_own(chips_sum(d_act_one)), from_own(gain_one_own), normed_one, inverse_one, d_resid
    )
    gain_parts = jnp.concatenate(
        [
            jnp.broadcast_to(gain_one_part[:, None], (features, HEAD // 2)),
            jnp.broadcast_to(gain_two_part[:, None], (features, HEAD // 2)),
        ],
        axis=1,
    )
    qkv_grad = to_chips(
        own_reduce(jnp.concatenate([matmul_rows(act_one, d_qkv), gain_parts], axis=1))
    ).astype(F32)

    def whole_columns(first):
        part = qkv_grad[..., first : first + head_width]
        return part.transpose(1, 0, 2).reshape(weight_rows, features)

    gain_grads = jnp.sum(qkv_grad[..., 3 * head_width :], axis=0)
    out_part = matmul_rows(mixed_low, d_attn)
    out_half = head_width // CORES
    out_sum = core_reduce(out_part[:out_half], out_part[out_half:])
    out_grad = batch_scatter(out_sum.astype(LOW), 0).astype(F32)

    return (
        block_out[None],
        tokens_grad[None],
        gain_grads[:, 0],
        whole_columns(0),
        whole_columns(head_width),
        whole_columns(2 * head_width),
        out_grad,
        gain_grads[:, HEAD // 2],
        gate_grad,
        up_grad,
        down_grad,
    )


def solution(mesh):
    rows = P(("seq", "batch"), None)
    vector = P(("seq", "batch"))
    cells = P("batch", "seq", None)
    return jax.shard_map(
        per_device,
        mesh=mesh,
        in_specs=(cells, cells, P("batch", "seq"))
        + (vector, rows, rows, rows, rows, vector, rows, rows, rows),
        out_specs=(cells, cells, vector, rows, rows, rows, rows, vector, rows, rows, rows),
        check_vma=False,
    )
```

```python
import functools

import jax
import jax.numpy as jnp
from jax import lax
from jax.experimental import pallas as pl
from jax.experimental.pallas import tpu as pltpu
from jax.sharding import PartitionSpec as P

HEAD = 128
WINDOW = 64
GPS = 4
CORES = 2

EPS = 1e-05
NEGATIVE = -1e30
ROWS_DIMS = (((0,), (0,)), ((), ()))
COLS_DIMS = (((1,), (1,)), ((), ()))
BLOCK = 128
ROWS = 64
LANES = 128
F32 = jnp.float32
LOW = jnp.bfloat16


def matmul(left, right):
    return jnp.dot(left, right, preferred_element_type=F32)


def matmul_rows(left, right):
    return lax.dot_general(left, right, ROWS_DIMS, preferred_element_type=F32)


def matmul_cols(left, right):
    return lax.dot_general(left, right, COLS_DIMS, preferred_element_type=F32)


def exchange(value, flip):
    count = lax.axis_size("seq")
    return lax.ppermute(value, "seq", [(place, place ^ flip) for place in range(count)])


def swap_core(value):
    return exchange(value, 1)


def chip_count():
    return lax.axis_size("seq") // CORES


def own_chip():
    return lax.axis_index("seq") // CORES


def own_core():
    return lax.axis_index("seq") % CORES


def gather_near(value):
    if chip_count() != 4:
        return [exchange(value, CORES * k) for k in range(1, chip_count())]
    return [exchange(value, CORES), exchange(value, 2 * CORES)]


def gather_far(near):
    if chip_count() != 4:
        return []
    half = near[0].shape[0] // 2
    return [exchange(near[0][:half], 2 * CORES), exchange(near[1][half:], CORES)]


def gathered_rows(value, near, far):
    return jnp.concatenate([value] + near + far, axis=0)


def chips_scatter(blocks):
    return [blocks[0]] + [exchange(blocks[k], CORES * k) for k in range(1, chip_count())]


def chips_sum_near(parts):
    if chip_count() != 4:
        blocks = parts[0].reshape((chip_count(), -1) + parts[0].shape[1:])
        return chips_scatter([blocks[k] for k in range(chip_count())])
    return [exchange(parts[1], CORES), exchange(parts[2], 2 * CORES)]


def chips_sum_far(parts, near):
    if chip_count() != 4:
        return []
    on_second = (parts[3].astype(F32) + near[0][1].astype(F32)).astype(LOW)
    on_first = (parts[4].astype(F32) + near[1][1].astype(F32)).astype(LOW)
    return [exchange(on_second, 2 * CORES), exchange(on_first, CORES)]


def summands(parts, near, far):
    if not far:
        return near, []
    return [parts[0]], [(near[0][0], near[1][0]), tuple(far)]


def summed(parts, near, far):
    wholes, pairs = summands(parts, near, far)
    total = sum(part.astype(F32) for part in wholes)
    return total + sum(jnp.concatenate(pair, axis=0).astype(F32) for pair in pairs)


def spread_shapes(chips, rows, columns):
    if chips != 4:
        return [(rows, columns)]
    tall, low = rows // chips, rows // chips // 2
    return [(tall, columns), (2, low, columns), (2, low, columns), (low, columns), (low, columns)]


def spread_block(block, value, outs, place=slice(None)):
    own, first, second, keep_second, keep_first = outs
    low = value.shape[0] // 2
    if block == 0:
        own[:, place] = value
    if block == 1:
        first[0, :, place] = value[:low]
        keep_first[:, place] = value[low:]
    if block == 2:
        keep_second[:, place] = value[:low]
        second[0, :, place] = value[low:]
    if block == 3:
        first[1, :, place] = value[:low]
        second[1, :, place] = value[low:]


def spread_step(step, value, outs, place=slice(None)):
    if len(outs) == 1:
        outs[0][:, place] = value
        return
    for block in range(4):

        @pl.when(step == block)
        def _():
            spread_block(block, value, outs, place)


def in_order(blocks):
    chip = own_chip()
    bit = 1
    while bit < len(blocks):
        flipped = (chip & bit) > 0
        blocks = [jnp.where(flipped, blocks[i ^ bit], blocks[i]) for i in range(len(blocks))]
        bit *= 2
    return blocks


def to_chips(value):
    chip = own_chip()
    blocks = [
        lax.dynamic_index_in_dim(value, chip ^ k, axis=0, keepdims=False)
        for k in range(chip_count())
    ]
    return jnp.stack(in_order(chips_scatter(blocks)))


def after(value, *others):
    return lax.optimization_barrier((value,) + others)[0]


def seq_sum(value):
    bit = 1
    while bit < lax.axis_size("seq"):
        value = value + exchange(value, bit)
        bit *= 2
    return value


def own_first(first, second):
    flipped = own_core() > 0
    return jnp.where(flipped, second, first), jnp.where(flipped, first, second)


def core_rows(mine, other):
    return jnp.concatenate(own_first(mine, other), axis=0)


def batch_gather(value, axis):
    return lax.all_gather(value, "batch", axis=axis, tiled=True)


def batch_scatter(value, axis):
    return lax.psum_scatter(value, "batch", scatter_dimension=axis, tiled=True)


FREE = pl.CostEstimate(flops=0, bytes_accessed=0, transcendentals=0)


def params(megabytes=32):
    return pltpu.CompilerParams(vmem_limit_bytes=megabytes * 2**20)


def whole(shape):
    return pl.BlockSpec(shape, lambda *step: (0,) * len(shape))


SCALAR = pl.BlockSpec(memory_space=pltpu.SMEM)


def own_columns(values, flipped, chips):
    width = values.shape[1] // (chips * CORES)
    cells = [values[:, i * width : (i + 1) * width] for i in range(chips * CORES)]
    mine = [jnp.where(flipped, cells[2 * q + 1], cells[2 * q]) for q in range(chips)]
    other = [jnp.where(flipped, cells[2 * q], cells[2 * q + 1]) for q in range(chips)]
    return jnp.concatenate(mine + other, axis=1)


def natural_columns(values, flipped, chips):
    width = values.shape[1] // (chips * CORES)
    cells = [values[:, i * width : (i + 1) * width] for i in range(chips * CORES)]
    pairs = []
    for q in range(chips):
        mine, other = cells[q], cells[chips + q]
        pairs += [jnp.where(flipped, other, mine), jnp.where(flipped, mine, other)]
    return jnp.concatenate(pairs, axis=1)


def project_kernel(chips, core, tokens, gain, mine, other, act, out):
    flipped = core[0] > 0
    half, columns = mine.shape[0], out.shape[1]

    @pl.loop(0, tokens.shape[0], step=ROWS)
    def _(start):
        rows = pl.ds(pl.multiple_of(start, ROWS), ROWS)
        values = tokens[rows, :].astype(F32)
        inverse = lax.rsqrt(jnp.mean(values * values, axis=-1, keepdims=True) + EPS)
        act[rows, :] = (own_columns(values * inverse, flipped, chips) * gain[...]).astype(LOW)

    total = matmul(act[:, :half], mine[:, :columns]) + matmul(act[:, half:], other[:, :columns])
    out[...] = total.astype(LOW)


def project(core, tokens, gain, mine, other, columns, chips):
    rows, features = tokens.shape
    tall = rows // chips
    return pl.pallas_call(
        functools.partial(project_kernel, chips),
        grid=(chips,),
        in_specs=[
            SCALAR,
            pl.BlockSpec((tall, features), lambda i: (i, 0)),
            whole(gain.shape),
            whole(mine.shape),
            whole(other.shape),
        ],
        out_specs=[
            pl.BlockSpec((tall, features), lambda i: (i, 0)),
            pl.BlockSpec((tall, columns), lambda i: (i, 0)),
        ],
        out_shape=[
            jax.ShapeDtypeStruct((rows, features), LOW),
            jax.ShapeDtypeStruct((rows, columns), LOW),
        ],
        compiler_params=params(40),
        cost_estimate=FREE,
    )(core, tokens, gain, mine, other)


def windows(keys, rim, step):
    if step == 0:
        return jnp.concatenate([rim, keys[:BLOCK]], axis=0)
    return keys[step * BLOCK - WINDOW : (step + 1) * BLOCK]


def window_probs(queries, keys, first, preceded):
    scores = matmul_cols(queries, keys) * HEAD ** (-0.5)
    query = lax.broadcasted_iota(jnp.int32, scores.shape, 0)
    key = lax.broadcasted_iota(jnp.int32, scores.shape, 1)
    allowed = (key > query) & (key <= query + WINDOW)
    if first:
        allowed = allowed & ((key >= WINDOW) | (preceded > 0))
    scores = jnp.where(allowed, scores, NEGATIVE)
    expo = jnp.exp(scores - jnp.max(scores, axis=-1, keepdims=True))
    return expo / jnp.sum(expo, axis=-1, keepdims=True)


def attend_kernel(core, preceded, qkv, rim, out):
    flipped = core[0] > 0
    ready = preceded[pl.program_id(0)]
    width = out.shape[2]
    heads = width // HEAD
    mixed = []
    for head in range(heads):
        cell = slice(head * HEAD, (head + 1) * HEAD)
        queries, keys, values = (
            qkv[0, :, part * width + head * HEAD : part * width + (head + 1) * HEAD]
            for part in range(3)
        )
        rim_keys = rim[0, :, cell]
        rim_values = rim[0, :, width + head * HEAD : width + (head + 1) * HEAD]
        rows = []
        for step in range(queries.shape[0] // BLOCK):
            probs = window_probs(
                queries[step * BLOCK : (step + 1) * BLOCK],
                windows(keys, rim_keys, step),
                step == 0,
                ready,
            )
            rows.append(matmul(probs.astype(LOW), windows(values, rim_values, step)))
        mixed.append(jnp.concatenate(rows, axis=0).astype(LOW))
    half = heads // CORES
    for head in range(half):
        first, second = mixed[head], mixed[half + head]
        out[0, :, head * HEAD : (head + 1) * HEAD] = jnp.where(flipped, second, first)
        out[0, :, (half + head) * HEAD : (half + head + 1) * HEAD] = jnp.where(
            flipped, first, second
        )


def attention(core, preceded, qkv, rims):
    chips, rows, columns = qkv.shape
    width = columns // 3
    return pl.pallas_call(
        attend_kernel,
        grid=(chips,),
        in_specs=[
            SCALAR,
            SCALAR,
            pl.BlockSpec((1, rows, columns), lambda i: (i, 0, 0)),
            pl.BlockSpec((1,) + rims.shape[1:], lambda i: (i, 0, 0)),
        ],
        out_specs=pl.BlockSpec((1, rows, width), lambda i: (i, 0, 0)),
        out_shape=jax.ShapeDtypeStruct((chips, rows, width), LOW),
        compiler_params=params(),
        cost_estimate=FREE,
    )(core, preceded, qkv, rims)


def attend_back_kernel(core, preceded, qkv, rim, d_mixed, out, lent):
    flipped = core[0] > 0
    ready = preceded[pl.program_id(0)]
    width = d_mixed.shape[2]
    heads = width // HEAD
    half = heads // CORES
    factor = HEAD ** (-0.5)
    for head in range(heads):
        queries, keys, values = (
            qkv[0, :, part * width + head * HEAD : part * width + (head + 1) * HEAD]
            for part in range(3)
        )
        rim_keys = rim[0, :, head * HEAD : (head + 1) * HEAD]
        rim_values = rim[0, :, width + head * HEAD : width + (head + 1) * HEAD]
        there = (head + half) % heads
        upstream = jnp.where(
            flipped,
            d_mixed[0, :, there * HEAD : (there + 1) * HEAD],
            d_mixed[0, :, head * HEAD : (head + 1) * HEAD],
        )
        steps = queries.shape[0] // BLOCK
        d_queries, d_keys, d_values = [], [], []
        for step in range(steps):
            rows = slice(step * BLOCK, (step + 1) * BLOCK)
            near_keys, near_values = windows(keys, rim_keys, step), windows(values, rim_values, step)
            probs = window_probs(queries[rows], near_keys, step == 0, ready)
            d_probs = matmul_cols(upstream[rows], near_values)
            d_scores = probs * (d_probs - jnp.sum(probs * d_probs, axis=-1, keepdims=True))
            d_scores = d_scores.astype(LOW)
            d_queries.append(matmul(d_scores, near_keys) * factor)
            d_keys.append(matmul_rows(d_scores, queries[rows]) * factor)
            d_values.append(matmul_rows(probs.astype(LOW), upstream[rows]))
        out[0, :, head * HEAD : (head + 1) * HEAD] = jnp.concatenate(d_queries, axis=0).astype(LOW)
        for part, grads in ((1, d_keys), (2, d_values)):
            first = (part - 1) * width + head * HEAD
            lent[0, :, first : first + HEAD] = grads[0][:WINDOW].astype(LOW)
            for step in range(steps):
                own = grads[step][WINDOW:]
                if step + 1 < steps:
                    keep = own[: BLOCK - WINDOW]
                    own = jnp.concatenate(
                        [keep, own[BLOCK - WINDOW :] + grads[step + 1][:WINDOW]], axis=0
                    )
                out[
                    0,
                    step * BLOCK : (step + 1) * BLOCK,
                    part * width + head * HEAD : part * width + (head + 1) * HEAD,
                ] = own.astype(LOW)


def attention_back(core, preceded, qkv, rims, d_mixed):
    chips, rows, columns = qkv.shape
    width = columns // 3
    return pl.pallas_call(
        attend_back_kernel,
        grid=(chips,),
        in_specs=[
            SCALAR,
            SCALAR,
            pl.BlockSpec((1, rows, columns), lambda i: (i, 0, 0)),
            pl.BlockSpec((1,) + rims.shape[1:], lambda i: (i, 0, 0)),
            pl.BlockSpec((1, rows, width), lambda i: (i, 0, 0)),
        ],
        out_specs=[
            pl.BlockSpec((1, rows, columns), lambda i: (i, 0, 0)),
            pl.BlockSpec((1,) + rims.shape[1:], lambda i: (i, 0, 0)),
        ],
        out_shape=[
            jax.ShapeDtypeStruct(qkv.shape, LOW),
            jax.ShapeDtypeStruct(rims.shape, LOW),
        ],
        compiler_params=params(),
        cost_estimate=FREE,
    )(core, preceded, qkv, rims, d_mixed)


def out_kernel(chips, core, mixed, mine, other, tokens, gain, resid, act):
    step, steps = pl.program_id(0), pl.num_programs(0)
    flipped = core[0] > 0

    @pl.when(step == 0)
    def _():
        resid[...] = tokens[...].astype(F32)

    @pl.when(step < steps // 2)
    def _():
        resid[...] += matmul(mixed[...], mine[...])

    @pl.when(step >= steps // 2)
    def _():
        resid[...] += matmul(mixed[...], other[...])

    @pl.when(step == steps - 1)
    def _():
        @pl.loop(0, tokens.shape[0], step=ROWS)
        def _(start):
            rows = pl.ds(pl.multiple_of(start, ROWS), ROWS)
            values = resid[rows, :]
            inverse = lax.rsqrt(jnp.mean(values * values, axis=-1, keepdims=True) + EPS)
            normed = own_columns(values * inverse, flipped, chips)
            act[rows, :] = (normed * gain[...]).astype(LOW)


def out_project(core, mixed, mine, other, tokens, gain, chips):
    rows, features = tokens.shape
    depth = mine.shape[0] // chips
    return pl.pallas_call(
        functools.partial(out_kernel, chips),
        grid=(2 * chips,),
        in_specs=[
            SCALAR,
            pl.BlockSpec((rows, depth), lambda i: (0, i)),
            pl.BlockSpec((depth, features), lambda i: (jnp.minimum(i, chips - 1), 0)),
            pl.BlockSpec((depth, features), lambda i: (jnp.maximum(i - chips, 0), 0)),
            whole(tokens.shape),
            whole(gain.shape),
        ],
        out_specs=[whole(tokens.shape), whole(tokens.shape)],
        out_shape=[
            jax.ShapeDtypeStruct(tokens.shape, F32),
            jax.ShapeDtypeStruct(tokens.shape, LOW),
        ],
        compiler_params=params(),
        cost_estimate=FREE,
    )(core, mixed, mine, other, tokens, gain)


def row_specs(steps, wholes, pairs, features):
    half = steps // 2

    def spec(first, last, count):
        low = functools.partial(lambda first, last, i: jnp.clip(i - first, 0, last - 1), first, last)
        if count == 2:
            return pl.BlockSpec((ROWS, features), lambda i: (low(i), 0))
        return pl.BlockSpec((None, ROWS, features), lambda i: (0, low(i), 0))

    specs = [spec(0, steps, 2) for _ in wholes]
    for first, second in pairs:
        specs += [spec(0, half, first.ndim), spec(half, half, second.ndim)]
    return specs


def sum_rows(step, steps, count, refs):
    total = sum(ref[...].astype(F32) for ref in refs[:count])
    for i in range(count, len(refs), 2):
        part = jnp.where(step < steps // 2, refs[i][...], refs[i + 1][...])
        total = total + part.astype(F32)
    return total


def norm_back_rows(chips, flipped, d_act, values, gain, upstream):
    d_act = natural_columns(d_act, flipped, chips)
    inverse = lax.rsqrt(jnp.mean(values * values, axis=-1, keepdims=True) + EPS)
    normed = values * inverse
    scaled = d_act * natural_columns(gain, flipped, chips)
    result = upstream + inverse * (
        scaled - normed * jnp.mean(scaled * normed, axis=-1, keepdims=True)
    )
    return result, jnp.sum(d_act * normed, axis=0, keepdims=True)


def middle_kernel(chips, steps, count, size, core, *refs):
    parts, refs = refs[:size], refs[size:]
    resid, gain, d_final, mine, other, d_resid, d_attn, d_mixed, gain_part = refs
    step = pl.program_id(0)
    flipped = core[0] > 0
    tall = resid.shape[0]

    @pl.when(step < steps)
    def _():
        grad, part = norm_back_rows(
            chips,
            flipped,
            sum_rows(step, steps, count, parts),
            resid[...],
            gain[...],
            d_final[...],
        )
        d_resid[...] = grad
        d_attn[pl.ds(pl.multiple_of(step * tall, tall), tall), :] = grad.astype(LOW)

        @pl.when(step == 0)
        def _():
            gain_part[...] = part

        @pl.when(step > 0)
        def _():
            gain_part[...] += part

    @pl.when(step == steps)
    def _():
        gain_part[...] = own_columns(gain_part[...], flipped, chips)

    @pl.when((step >= steps) & (step < steps + chips))
    def _():
        d_mixed[0] = matmul_cols(d_attn[...], mine[...]).astype(LOW)

    @pl.when(step >= steps + chips)
    def _():
        d_mixed[0] = matmul_cols(d_attn[...], other[...]).astype(LOW)


def middle(core, wholes, pairs, resid, gain, d_final, mine, other, chips):
    parts = list(wholes) + [half for pair in pairs for half in pair]
    rows, features = resid.shape
    steps = rows // ROWS
    depth = mine.shape[0] // chips

    def by_rows():
        return pl.BlockSpec((ROWS, features), lambda i: (jnp.minimum(i, steps - 1), 0))

    return pl.pallas_call(
        functools.partial(middle_kernel, chips, steps, len(wholes), len(parts)),
        grid=(steps + 2 * chips,),
        in_specs=[SCALAR]
        + row_specs(steps, wholes, pairs, features)
        + [
            by_rows(),
            whole(gain.shape),
            by_rows(),
            pl.BlockSpec((depth, features), lambda i: (jnp.clip(i - steps, 0, chips - 1), 0)),
            pl.BlockSpec(
                (depth, features), lambda i: (jnp.clip(i - steps - chips, 0, chips - 1), 0)
            ),
        ],
        out_specs=[
            by_rows(),
            whole(resid.shape),
            pl.BlockSpec(
                (1, rows, depth),
                lambda i: (
                    lax.rem(jnp.maximum(i - steps, 0), chips),
                    0,
                    lax.div(jnp.maximum(i - steps, 0), chips),
                ),
            ),
            whole((1, features)),
        ],
        out_shape=[
            jax.ShapeDtypeStruct(resid.shape, F32),
            jax.ShapeDtypeStruct(resid.shape, LOW),
            jax.ShapeDtypeStruct((chips, rows, 2 * depth), LOW),
            jax.ShapeDtypeStruct((1, features), F32),
        ],
        compiler_params=params(),
        cost_estimate=FREE,
    )(core, *parts, resid, gain, d_final, mine, other)


def last_kernel(chips, steps, count, core, *refs):
    parts, refs = refs[:-4], refs[-4:]
    tokens, gain, d_resid, out = refs
    out[...], _ = norm_back_rows(
        chips,
        core[0] > 0,
        sum_rows(pl.program_id(0), steps, count, parts),
        tokens[...].astype(F32),
        gain[...],
        d_resid[...],
    )


def last(core, wholes, pairs, tokens, gain, d_resid, chips):
    parts = list(wholes) + [half for pair in pairs for half in pair]
    rows, features = tokens.shape
    steps = rows // ROWS
    by_rows = pl.BlockSpec((ROWS, features), lambda i: (i, 0))
    return pl.pallas_call(
        functools.partial(last_kernel, chips, steps, len(wholes)),
        grid=(steps,),
        in_specs=[SCALAR]
        + row_specs(steps, wholes, pairs, features)
        + [by_rows, whole(gain.shape), by_rows],
        out_specs=by_rows,
        out_shape=jax.ShapeDtypeStruct(tokens.shape, F32),
        compiler_params=params(),
        cost_estimate=FREE,
    )(core, *parts, tokens, gain, d_resid)


def inner_first_kernel(act, gate, upward, out):
    out[...] = matmul(act[...], jnp.concatenate([gate[...], upward[...]], axis=1))


def inner_second_kernel(act, gate, upward, first, hidden, slope_gate, slope_up):
    width = gate.shape[1]
    both = first[...] + matmul(act[...], jnp.concatenate([gate[...], upward[...]], axis=1))
    gate, upward = both[:, :width], both[:, width:]
    sigma = jax.nn.sigmoid(gate)
    silu = gate * sigma
    hidden[...] = (silu * upward).astype(LOW)
    slope_gate[...] = upward * sigma * (1.0 + gate * (1.0 - sigma))
    slope_up[...] = silu


def inner_specs(act, weights, part):
    rows = act.shape[0]
    half, columns = weights.shape
    tiles = columns // (2 * LANES)
    return tiles, [
        pl.BlockSpec((rows, half), lambda i: (0, part)),
        pl.BlockSpec((half, LANES), lambda i: (0, i)),
        pl.BlockSpec((half, LANES), lambda i: (0, tiles + i)),
    ]


def inner_first(act, weights):
    rows, columns = act.shape[0], weights.shape[1]
    if columns % (2 * LANES):
        return matmul(act[:, : weights.shape[0]], weights)
    tiles, specs = inner_specs(act, weights, 0)
    return pl.pallas_call(
        inner_first_kernel,
        grid=(tiles,),
        in_specs=specs,
        out_specs=pl.BlockSpec((rows, 2 * LANES), lambda i: (0, i)),
        out_shape=jax.ShapeDtypeStruct((rows, columns), F32),
        compiler_params=params(),
        cost_estimate=FREE,
    )(act, weights, weights)


def inner_second(act, weights, first):
    rows, columns = act.shape[0], weights.shape[1]
    width = columns // 2
    if columns % (2 * LANES):
        both = first + matmul(act[:, weights.shape[0] :], weights)
        gate, upward = both[:, :width], both[:, width:]
        sigma = jax.nn.sigmoid(gate)
        silu = gate * sigma
        return (silu * upward).astype(LOW), upward * sigma * (1.0 + gate * (1.0 - sigma)), silu
    tiles, specs = inner_specs(act, weights, 1)
    tile = pl.BlockSpec((rows, LANES), lambda i: (0, i))
    return pl.pallas_call(
        inner_second_kernel,
        grid=(tiles,),
        in_specs=specs + [pl.BlockSpec((rows, 2 * LANES), lambda i: (0, i))],
        out_specs=[tile] * 3,
        out_shape=[
            jax.ShapeDtypeStruct((rows, width), LOW),
            jax.ShapeDtypeStruct((rows, width), F32),
            jax.ShapeDtypeStruct((rows, width), F32),
        ],
        compiler_params=params(),
        cost_estimate=FREE,
    )(act, weights, weights, first)


def place_halves(flag, mine, other, out):
    rows = mine.shape[0]
    core = flag[0]
    out[pl.ds(pl.multiple_of(core * rows, 16), rows), :] = mine[...]
    out[pl.ds(pl.multiple_of((1 - core) * rows, 16), rows), :] = other[...]


def inner_back_kernel(flag, d_ffn, mine, other, slope_gate, slope_up, out, down):
    @pl.when(pl.program_id(0) == 0)
    def _():
        place_halves(flag, mine, other, down)

    width = down.shape[0]
    d_hidden = matmul_cols(d_ffn[...], down[...])
    out[:, :width] = (d_hidden * slope_gate[...]).astype(LOW)
    out[:, width:] = (d_hidden * slope_up[...]).astype(LOW)


def inner_back(flag, d_ffn, mine, other, slope_gate, slope_up, chips):
    rows, features = d_ffn.shape
    width = 2 * mine.shape[0]
    if width % LANES:
        d_hidden = matmul_cols(d_ffn, core_rows(mine, other))
        return jnp.concatenate([d_hidden * slope_gate, d_hidden * slope_up], axis=1).astype(LOW)
    tall = rows // chips
    flat = pl.BlockSpec((tall, width), lambda i: (i, 0))
    return pl.pallas_call(
        inner_back_kernel,
        grid=(chips,),
        in_specs=[
            SCALAR,
            pl.BlockSpec((tall, features), lambda i: (i, 0)),
            whole(mine.shape),
            whole(other.shape),
            flat,
            flat,
        ],
        out_specs=pl.BlockSpec((tall, 2 * width), lambda i: (i, 0)),
        out_shape=jax.ShapeDtypeStruct((rows, 2 * width), LOW),
        scratch_shapes=[pltpu.VMEM((width, features), LOW)],
        compiler_params=params(44),
        cost_estimate=FREE,
    )(flag, d_ffn, mine, other, slope_gate, slope_up)


def back_project_kernel(d_out, mine, other, act, total, *outs):
    half, columns = mine.shape[0], d_out.shape[1]
    step = pl.program_id(0)
    for place, weights in ((slice(0, half), mine), (slice(half, 2 * half), other)):
        grad = matmul_cols(d_out[...], weights[:, :columns])
        spread_step(step, grad.astype(LOW), outs, place)
        part = jnp.sum(grad * act[:, place].astype(F32), axis=0, keepdims=True)
        total[:, place] = part + jnp.where(step > 0, total[:, place], 0.0)


def back_project(d_out, mine, other, act, chips):
    rows, columns = d_out.shape
    features = 2 * mine.shape[0]
    tall = rows // chips
    shapes = spread_shapes(chips, rows, features)
    flat = pl.BlockSpec((tall, features), lambda i: (i, 0))
    total, *outs = pl.pallas_call(
        back_project_kernel,
        grid=(chips,),
        in_specs=[
            pl.BlockSpec((tall, columns), lambda i: (i, 0)),
            whole(mine.shape),
            whole(other.shape),
            flat,
        ],
        out_specs=[whole((1, features))]
        + ([flat] if len(shapes) == 1 else [whole(shape) for shape in shapes]),
        out_shape=[jax.ShapeDtypeStruct((1, features), F32)]
        + [jax.ShapeDtypeStruct(shape, LOW) for shape in shapes],
        compiler_params=params(48),
        cost_estimate=FREE,
    )(d_out, mine, other, act)
    return outs, total


def turned_kernel(count, left, right, *refs):
    arrived, outs = refs[:count], refs[count:]
    total = matmul_rows(left[...], right[...])
    if arrived:
        total = total + arrived[0][...].astype(F32)
    total = total.astype(LOW)
    if len(outs) == 1:
        outs[0][...] = total
        return
    tall = total.shape[0] // 4
    for block in range(4):
        spread_block(block, total[block * tall : (block + 1) * tall], outs)


def turned(left, part, right, *arrived, chips=1):
    rows, half = left.shape[0], left.shape[1] // CORES
    width = right.shape[1]
    tile = LANES if width % (2 * LANES) else 2 * LANES
    shapes = spread_shapes(chips, half, width)
    outs = pl.pallas_call(
        functools.partial(turned_kernel, len(arrived)),
        grid=(width // tile,),
        in_specs=[
            pl.BlockSpec((rows, half), lambda i: (0, part)),
            pl.BlockSpec((rows, tile), lambda i: (0, i)),
        ]
        + [pl.BlockSpec((half, tile), lambda i: (0, i)) for _ in arrived],
        out_specs=[
            pl.BlockSpec(shape[:-1] + (tile,), lambda i, n=len(shape): (0,) * (n - 1) + (i,))
            for shape in shapes
        ],
        out_shape=[jax.ShapeDtypeStruct(shape, LOW) for shape in shapes],
        compiler_params=params(),
        cost_estimate=FREE,
    )(left, right, *arrived)
    return outs[0] if chips == 1 else outs


def inner_out_kernel(flag, left, mine, other, *refs):
    outs, down = refs[:-1], refs[-1]
    step = pl.program_id(0)

    @pl.when(step == 0)
    def _():
        place_halves(flag, mine, other, down)

    spread_step(step, matmul(left[...], down[...]).astype(LOW), outs)


def inner_out(flag, hidden, mine, other, chips):
    rows, width = hidden.shape
    features = mine.shape[1]
    if width % LANES:
        return [matmul(hidden, core_rows(mine, other)).astype(LOW)]
    tall = rows // chips
    shapes = spread_shapes(chips, rows, features)
    flat = pl.BlockSpec((tall, features), lambda i: (i, 0))
    return pl.pallas_call(
        inner_out_kernel,
        grid=(chips,),
        in_specs=[
            SCALAR,
            pl.BlockSpec((tall, width), lambda i: (i, 0)),
            whole(mine.shape),
            whole(other.shape),
        ],
        out_specs=[flat] if len(shapes) == 1 else [whole(shape) for shape in shapes],
        out_shape=[jax.ShapeDtypeStruct(shape, LOW) for shape in shapes],
        scratch_shapes=[pltpu.VMEM((width, features), LOW)],
        compiler_params=params(36),
        cost_estimate=FREE,
    )(flag, hidden, mine, other)


def half_kernel(flag, left, right, *refs):
    arrived, out = refs[:-1], refs[-1]
    rows = out.shape[0]
    start = left.shape[1] - rows
    wide = -(-rows // LANES) * LANES
    second = flag[0] > 0
    first = pl.multiple_of(jnp.where(second, left.shape[1] - wide, 0), LANES)
    total = matmul_rows(left[:, pl.ds(first, wide)], right[...])
    total = jnp.where(second, total[wide - rows :], total[:rows])
    if arrived:
        total = total + arrived[0][...].astype(F32)
    out[...] = total.astype(LOW)


def half_product(flag, left, right, *arrived):
    rows, columns = left.shape
    width = right.shape[1]
    half = columns // 2
    if columns % LANES:
        total = matmul_rows(left, right)
        total = jnp.where(flag[0] > 0, total[half:], total[:half])
        return sum([part.astype(F32) for part in arrived], total).astype(LOW)
    tile = 2 * LANES
    return pl.pallas_call(
        half_kernel,
        grid=(width // tile,),
        in_specs=[SCALAR, whole(left.shape), pl.BlockSpec((rows, tile), lambda i: (0, i))]
        + [pl.BlockSpec((half, tile), lambda i: (0, i)) for _ in arrived],
        out_specs=pl.BlockSpec((half, tile), lambda i: (0, i)),
        out_shape=jax.ShapeDtypeStruct((half, width), LOW),
        compiler_params=params(),
        cost_estimate=FREE,
    )(flag, left, right, *arrived)


def per_device(
    tokens,
    out_cotangent,
    group_ids,
    attn_gain,
    query_weight,
    key_weight,
    value_weight,
    out_weight,
    ffn_gain,
    gate_weight,
    up_weight,
    down_weight,
):
    tok_count, features = tokens.shape[1:]
    weight_rows, inner = gate_weight.shape
    chips = chip_count()
    chip, core = own_chip(), own_core()
    ids = lax.iota(jnp.int32, chips)
    head_width, inner_width = features // chips, inner // chips
    half = features // CORES
    flag = jnp.full((1,), core, jnp.int32)
    tokens, out_cotangent = tokens[0], out_cotangent[0]

    gains = jnp.concatenate(
        [
            jnp.broadcast_to(attn_gain[:, None], (weight_rows, LANES // 2)),
            jnp.broadcast_to(ffn_gain[:, None], (weight_rows, LANES // 2)),
        ],
        axis=1,
    )

    def for_chip(weight, k):
        width = weight.shape[1] // chips
        return lax.dynamic_slice_in_dim(weight, (chip ^ k) * width, width, axis=1)

    def rows_of_chips(weights, *others):
        parts = [jnp.concatenate([for_chip(w, k) for w in weights], axis=1) for k in range(chips)]
        parts = [jnp.concatenate([part] + list(others), axis=1) for part in parts]
        return jnp.stack(in_order(chips_scatter(parts)))

    group_span = GPS * lax.axis_size("batch")
    onehot = (group_ids[0, :, None] == jnp.arange(group_span, dtype=jnp.int32)[None, :]).astype(F32)
    group_total = seq_sum(jnp.sum(onehot, axis=0, keepdims=True))
    own_total = jnp.sum(onehot * group_total, axis=-1)[:, None]
    weighting = tok_count * lax.axis_size("seq") / (GPS * own_total)
    d_final = out_cotangent.astype(F32) * weighting

    out_mine = batch_gather(out_weight, 0)
    qkv_rows = rows_of_chips([query_weight, key_weight, value_weight], gains)
    qkv_mine = batch_gather(after(qkv_rows, out_mine), 1).reshape(half, -1)
    tokens_sent = after(tokens, qkv_rows, group_total)
    tokens_near = gather_near(tokens_sent)
    tokens_far = gather_far(tokens_near)
    gathered = gathered_rows(tokens_sent, tokens_near, tokens_far)
    gate_weight, up_weight = after((gate_weight, up_weight), *tokens_near, *tokens_far)
    inner_rows = rows_of_chips([gate_weight, up_weight])
    inner_mine = batch_gather(inner_rows, 1).reshape(half, -1)
    down_mine = batch_gather(after(down_weight, inner_rows), 0)

    out_sent = after(out_mine, inner_rows)
    out_near = gather_near(out_sent)
    qkv_mine = after(qkv_mine, *out_near)
    qkv_other = swap_core(qkv_mine)
    out_far = gather_far(out_near)
    qkv_other = after(qkv_other, *out_far)
    columns = 3 * head_width
    gain_one, gain_two = (
        jnp.concatenate([qkv_mine[:, place], qkv_other[:, place]]).astype(F32)[None]
        for place in (columns, columns + LANES // 2)
    )
    act_one, qkv = project(flag, gathered, gain_one, qkv_mine, qkv_other, columns, chips)
    qkv = qkv.reshape(chips, tok_count, columns)
    ffn_sent = after(d_final.astype(LOW), *out_far)
    ffn_near = gather_near(ffn_sent)
    place = chip ^ ids
    tails = swap_core(qkv[:, tok_count - WINDOW :, head_width:])
    ffn_far = gather_far(ffn_near)
    before = jnp.where(core > 0, ids, chip ^ jnp.maximum(place - 1, 0))
    follow = jnp.where(core > 0, chip ^ jnp.minimum(place + 1, chips - 1), ids)
    preceded = ((core > 0) | (place > 0)).astype(jnp.int32)
    followed = (core == 0) | (place < chips - 1)
    rims = jnp.take(after(tails, *ffn_near), before, axis=0)
    mixed = attention(flag, preceded, qkv, rims)

    mixed = after(mixed, *ffn_far)
    mixed_own = chips_scatter([mixed[k] for k in range(chips)])
    cell = head_width // CORES
    mixed_own = jnp.concatenate(
        [block[:, i * cell : (i + 1) * cell] for i in range(CORES) for block in mixed_own], axis=1
    )
    out_near = after(out_near, mixed)
    out_half = gathered_rows(out_sent, out_near, out_far)
    out_other = swap_core(out_half)
    resid, act_two_own = out_project(
        flag, mixed_own, out_half, out_other, tokens, gain_two, chips
    )

    act_near = gather_near(act_two_own)
    act_far = gather_far(act_near)
    act_two = gathered_rows(act_two_own, act_near, act_far)
    d_ffn = gathered_rows(ffn_sent, after(ffn_near, act_two_own), ffn_far)
    inner_mine = after(inner_mine, *act_near, *act_far)
    inner_other = swap_core(inner_mine)
    hidden, slope_gate, slope_up = inner_second(
        act_two, inner_other, inner_first(act_two, inner_mine)
    )
    down_send = half_product(1 - flag, hidden, d_ffn)
    down_back = swap_core(down_send)
    down_sum = half_product(flag, hidden, after(d_ffn, down_send), down_back)
    down_mine = after(down_mine, down_sum)
    down_other = swap_core(down_mine)
    down_grad = batch_scatter(down_sum, 0)
    d_gate_up = inner_back(
        flag, after(d_ffn, down_sum), down_mine, down_other, slope_gate, slope_up, chips
    )
    inner_send = turned(act_two, 1, d_gate_up)
    act_parts, _ = back_project(
        after(d_gate_up, inner_send), inner_mine, inner_other, act_two, chips
    )
    act_near = chips_sum_near(act_parts)
    inner_sum = turned(
        act_two, 0, after(d_gate_up, act_parts[0], down_grad), swap_core(inner_send)
    )
    act_far = chips_sum_far(act_parts, act_near)
    inner_sum = after(inner_sum, *act_near)
    inner_grad = batch_scatter(inner_sum.reshape(chips, half // chips, -1), 1)
    d_resid, d_attn, d_mixed_own, gain_two_part = middle(
        flag,
        *summands(act_parts, act_near, act_far),
        resid,
        gain_two,
        d_final,
        out_half,
        out_other,
        chips,
    )

    d_mixed_parts = chips_scatter([d_mixed_own[k] for k in range(chips)])
    d_mixed = jnp.stack(d_mixed_parts)
    d_qkv, lent = attention_back(flag, preceded, qkv, rims, d_mixed)
    lent = swap_core(lent)
    block_parts = inner_out(flag, after(hidden, d_mixed_own), down_mine, down_other, chips)
    block_near = chips_sum_near(block_parts)

    returned = jnp.where(followed[:, None, None], jnp.take(lent, follow, axis=0), 0)
    d_qkv = d_qkv.at[:, tok_count - WINDOW :, head_width:].add(returned)
    d_qkv = after(d_qkv.reshape(chips * tok_count, columns), *block_near)
    block_far = chips_sum_far(block_parts, block_near)
    qkv_send = turned(act_one, 1, d_qkv)
    out_send = turned(mixed_own, 1, after(d_attn, qkv_send))
    qkv_sum = turned(act_one, 0, after(d_qkv, out_send), swap_core(qkv_send))
    out_parts = turned(mixed_own, 0, after(d_attn, qkv_sum), swap_core(out_send), chips=chips)
    if chips == 1:
        out_parts = [out_parts]
    out_parts = after(out_parts, *block_far)
    out_near = chips_sum_near(out_parts)
    out_far = chips_sum_far(out_parts, out_near)
    d_act_parts, gain_one_part = back_project(
        after(d_qkv, out_parts[0]), qkv_mine, qkv_other, act_one, chips
    )
    gain_one_part = gain_one_part / gain_one
    gain_parts = jnp.concatenate(
        [
            jnp.broadcast_to(part.reshape(features, 1), (features, LANES // 2))
            for part in (gain_one_part, gain_two_part)
        ],
        axis=1,
    )
    d_act_parts = after(d_act_parts, *out_far)
    d_act_near = chips_sum_near(d_act_parts)
    d_act_far = chips_sum_far(d_act_parts, d_act_near)
    gain_sum = gain_parts[:half] + swap_core(gain_parts[half:].astype(LOW)).astype(F32)
    qkv_sum = jnp.concatenate([qkv_sum, gain_sum.astype(LOW)], axis=1)
    qkv_sum = after(qkv_sum, inner_grad)
    qkv_grad = batch_scatter(qkv_sum.reshape(chips, half // chips, -1), 1)
    out_sum = summed(out_parts, out_near, out_far).astype(LOW)
    out_grad = batch_scatter(after(out_sum, qkv_grad), 0)
    tokens_grad = last(
        flag, *summands(d_act_parts, d_act_near, d_act_far), tokens, gain_one, d_resid, chips
    )
    block_out = (resid + summed(block_parts, block_near, block_far)).astype(LOW)

    def columns_of_chips(grad):
        chip_rows = [
            lax.dynamic_index_in_dim(grad, chip ^ k, axis=0, keepdims=False) for k in range(chips)
        ]
        return in_order(chips_scatter(chip_rows))

    inner_grad = columns_of_chips(inner_grad)
    qkv_grad = columns_of_chips(qkv_grad)

    def whole_columns(blocks, first, width):
        parts = [block[:, first : first + width] for block in blocks]
        return jnp.concatenate(parts, axis=1).astype(F32)

    gain_grads = sum(block[:, columns:].astype(F32) for block in qkv_grad)

    return (
        block_out[None],
        tokens_grad[None],
        gain_grads[:, 0],
        whole_columns(qkv_grad, 0, head_width),
        whole_columns(qkv_grad, head_width, head_width),
        whole_columns(qkv_grad, 2 * head_width, head_width),
        out_grad.astype(F32),
        gain_grads[:, LANES // 2],
        whole_columns(inner_grad, 0, inner_width),
        whole_columns(inner_grad, inner_width, inner_width),
        down_grad.astype(F32),
    )


def solution(mesh):
    rows = P(("seq", "batch"), None)
    vector = P(("seq", "batch"))
    cells = P("batch", "seq", None)
    return jax.shard_map(
        per_device,
        mesh=mesh,
        in_specs=(cells, cells, P("batch", "seq"))
        + (vector, rows, rows, rows, rows, vector, rows, rows, rows),
        out_specs=(cells, cells, vector, rows, rows, rows, rows, vector, rows, rows, rows),
        check_vma=False,
    )
```

```python
import functools

import jax
import jax.numpy as jnp
from jax import lax
from jax.experimental import pallas as pl
from jax.experimental.pallas import tpu as pltpu
from jax.sharding import PartitionSpec as P

HEAD = 128
WINDOW = 64
GPS = 4
CORES = 2

EPS = 1e-05
NEGATIVE = -1e30
ROWS_DIMS = (((0,), (0,)), ((), ()))
COLS_DIMS = (((1,), (1,)), ((), ()))
BLOCK = 128
ROWS = 64
LANES = 128
F32 = jnp.float32
LOW = jnp.bfloat16


def matmul(left, right):
    return jnp.dot(left, right, preferred_element_type=F32)


def matmul_rows(left, right):
    return lax.dot_general(left, right, ROWS_DIMS, preferred_element_type=F32)


def matmul_cols(left, right):
    return lax.dot_general(left, right, COLS_DIMS, preferred_element_type=F32)


def exchange(value, flip, axis="seq"):
    if flip == 0:
        return value
    count = lax.axis_size(axis)
    return lax.ppermute(value, axis, [(place, place ^ flip) for place in range(count)])


def swap_core(value):
    return exchange(value, 1)


def chip_count():
    return lax.axis_size("seq") // CORES


def own_chip():
    return lax.axis_index("seq") // CORES


def own_core():
    return lax.axis_index("seq") % CORES


def gather_near(value):
    if chip_count() != 4:
        return [exchange(value, CORES * k) for k in range(1, chip_count())]
    return [exchange(value, CORES), exchange(value, 2 * CORES)]


def gather_far(near):
    if chip_count() != 4:
        return []
    half = near[0].shape[0] // 2
    return [exchange(near[0][:half], 2 * CORES), exchange(near[1][half:], CORES)]


def gathered_rows(value, near, far):
    return jnp.concatenate([value] + near + far, axis=0)


def chips_scatter(blocks):
    return [blocks[0]] + [exchange(blocks[k], CORES * k) for k in range(1, chip_count())]


def chips_sum_near(parts):
    if chip_count() != 4:
        blocks = parts[0].reshape((chip_count(), -1) + parts[0].shape[1:])
        return chips_scatter([blocks[k] for k in range(chip_count())])
    return [exchange(parts[1], CORES), exchange(parts[2], 2 * CORES)]


def chips_sum_far(parts, near):
    if chip_count() != 4:
        return []
    on_second = (parts[3].astype(F32) + near[0][1].astype(F32)).astype(LOW)
    on_first = (parts[4].astype(F32) + near[1][1].astype(F32)).astype(LOW)
    return [exchange(on_second, 2 * CORES), exchange(on_first, CORES)]


def summands(parts, near, far):
    if not far:
        return near, []
    return [parts[0]], [(near[0][0], near[1][0]), tuple(far)]


def summed(parts, near, far):
    wholes, pairs = summands(parts, near, far)
    total = sum(part.astype(F32) for part in wholes)
    return total + sum(jnp.concatenate(pair, axis=0).astype(F32) for pair in pairs)


def spread_shapes(chips, rows, columns):
    if chips != 4:
        return [(rows, columns)]
    tall, low = rows // chips, rows // chips // 2
    return [(tall, columns), (2, low, columns), (2, low, columns), (low, columns), (low, columns)]


def spread_block(block, value, outs, place=slice(None)):
    own, first, second, keep_second, keep_first = outs
    low = value.shape[0] // 2
    if block == 0:
        own[:, place] = value
    if block == 1:
        first[0, :, place] = value[:low]
        keep_first[:, place] = value[low:]
    if block == 2:
        keep_second[:, place] = value[:low]
        second[0, :, place] = value[low:]
    if block == 3:
        first[1, :, place] = value[:low]
        second[1, :, place] = value[low:]


def spread(total, outs):
    if len(outs) == 1:
        outs[0][...] = total
        return
    tall = total.shape[0] // 4
    for block in range(4):
        spread_block(block, total[block * tall : (block + 1) * tall], outs)


def column_spec(shape, tile):
    lead = (0,) * (len(shape) - 1)
    return pl.BlockSpec(shape[:-1] + (tile,), lambda i: lead + (i,))


def spread_step(step, value, outs, place=slice(None)):
    if len(outs) == 1:
        outs[0][:, place] = value
        return
    for block in range(4):

        @pl.when(step == block)
        def _():
            spread_block(block, value, outs, place)


def in_order(blocks):
    chip = own_chip()
    bit = 1
    while bit < len(blocks):
        flipped = (chip & bit) > 0
        blocks = [jnp.where(flipped, blocks[i ^ bit], blocks[i]) for i in range(len(blocks))]
        bit *= 2
    return blocks


def to_chips(value):
    chip = own_chip()
    blocks = [
        lax.dynamic_index_in_dim(value, chip ^ k, axis=0, keepdims=False)
        for k in range(chip_count())
    ]
    return jnp.stack(in_order(chips_scatter(blocks)))


def after(value, *others):
    return lax.optimization_barrier((value,) + others)[0]


def seq_sum(value):
    bit = 1
    while bit < lax.axis_size("seq"):
        value = value + exchange(value, bit)
        bit *= 2
    return value


def own_first(first, second):
    flipped = own_core() > 0
    return jnp.where(flipped, second, first), jnp.where(flipped, first, second)


def core_rows(mine, other):
    return jnp.concatenate(own_first(mine, other), axis=0)


def batch_gather(value, axis):
    return lax.all_gather(value, "batch", axis=axis, tiled=True)


def batch_scatter(value, axis):
    return lax.psum_scatter(value, "batch", scatter_dimension=axis, tiled=True)


FREE = pl.CostEstimate(flops=0, bytes_accessed=0, transcendentals=0)


def params(megabytes=32):
    return pltpu.CompilerParams(vmem_limit_bytes=megabytes * 2**20)


def whole(shape):
    return pl.BlockSpec(shape, lambda *step: (0,) * len(shape))


SCALAR = pl.BlockSpec(memory_space=pltpu.SMEM)


def own_columns(values, flipped, chips):
    width = values.shape[1] // (chips * CORES)
    cells = [values[:, i * width : (i + 1) * width] for i in range(chips * CORES)]
    mine = [jnp.where(flipped, cells[2 * q + 1], cells[2 * q]) for q in range(chips)]
    other = [jnp.where(flipped, cells[2 * q], cells[2 * q + 1]) for q in range(chips)]
    return jnp.concatenate(mine + other, axis=1)


def natural_columns(values, flipped, chips):
    width = values.shape[1] // (chips * CORES)
    cells = [values[:, i * width : (i + 1) * width] for i in range(chips * CORES)]
    pairs = []
    for q in range(chips):
        mine, other = cells[q], cells[chips + q]
        pairs += [jnp.where(flipped, other, mine), jnp.where(flipped, mine, other)]
    return jnp.concatenate(pairs, axis=1)


def project_kernel(chips, core, tokens, gain, mine, other, act, out):
    flipped = core[0] > 0
    half, columns = mine.shape[0], out.shape[1]

    @pl.loop(0, tokens.shape[0], step=ROWS)
    def _(start):
        rows = pl.ds(pl.multiple_of(start, ROWS), ROWS)
        values = tokens[rows, :].astype(F32)
        inverse = lax.rsqrt(jnp.mean(values * values, axis=-1, keepdims=True) + EPS)
        act[rows, :] = (own_columns(values * inverse, flipped, chips) * gain[...]).astype(LOW)

    total = matmul(act[:, :half], mine[:, :columns]) + matmul(act[:, half:], other[:, :columns])
    out[...] = total.astype(LOW)


def project(core, tokens, gain, mine, other, columns, chips):
    rows, features = tokens.shape
    tall = rows // chips
    return pl.pallas_call(
        functools.partial(project_kernel, chips),
        grid=(chips,),
        in_specs=[
            SCALAR,
            pl.BlockSpec((tall, features), lambda i: (i, 0)),
            whole(gain.shape),
            whole(mine.shape),
            whole(other.shape),
        ],
        out_specs=[
            pl.BlockSpec((tall, features), lambda i: (i, 0)),
            pl.BlockSpec((tall, columns), lambda i: (i, 0)),
        ],
        out_shape=[
            jax.ShapeDtypeStruct((rows, features), LOW),
            jax.ShapeDtypeStruct((rows, columns), LOW),
        ],
        compiler_params=params(40),
        cost_estimate=FREE,
    )(core, tokens, gain, mine, other)


def windows(keys, rim, step):
    if step == 0:
        return jnp.concatenate([rim, keys[:BLOCK]], axis=0)
    return keys[step * BLOCK - WINDOW : (step + 1) * BLOCK]


def window_probs(queries, keys, first, preceded):
    scores = matmul_cols(queries, keys) * HEAD ** (-0.5)
    query = lax.broadcasted_iota(jnp.int32, scores.shape, 0)
    key = lax.broadcasted_iota(jnp.int32, scores.shape, 1)
    allowed = (key > query) & (key <= query + WINDOW)
    if first:
        allowed = allowed & ((key >= WINDOW) | (preceded > 0))
    scores = jnp.where(allowed, scores, NEGATIVE)
    expo = jnp.exp(scores - jnp.max(scores, axis=-1, keepdims=True))
    return expo / jnp.sum(expo, axis=-1, keepdims=True)


def attend_kernel(core, preceded, qkv, rim, out):
    flipped = core[0] > 0
    ready = preceded[pl.program_id(0)]
    width = out.shape[2]
    heads = width // HEAD
    mixed = []
    for head in range(heads):
        cell = slice(head * HEAD, (head + 1) * HEAD)
        queries, keys, values = (
            qkv[0, :, part * width + head * HEAD : part * width + (head + 1) * HEAD]
            for part in range(3)
        )
        rim_keys = rim[0, :, cell]
        rim_values = rim[0, :, width + head * HEAD : width + (head + 1) * HEAD]
        rows = []
        for step in range(queries.shape[0] // BLOCK):
            probs = window_probs(
                queries[step * BLOCK : (step + 1) * BLOCK],
                windows(keys, rim_keys, step),
                step == 0,
                ready,
            )
            rows.append(matmul(probs.astype(LOW), windows(values, rim_values, step)))
        mixed.append(jnp.concatenate(rows, axis=0).astype(LOW))
    half = heads // CORES
    for head in range(half):
        first, second = mixed[head], mixed[half + head]
        out[0, :, head * HEAD : (head + 1) * HEAD] = jnp.where(flipped, second, first)
        out[0, :, (half + head) * HEAD : (half + head + 1) * HEAD] = jnp.where(
            flipped, first, second
        )


def attention(core, preceded, qkv, rims):
    chips, rows, columns = qkv.shape
    width = columns // 3
    return pl.pallas_call(
        attend_kernel,
        grid=(chips,),
        in_specs=[
            SCALAR,
            SCALAR,
            pl.BlockSpec((1, rows, columns), lambda i: (i, 0, 0)),
            pl.BlockSpec((1,) + rims.shape[1:], lambda i: (i, 0, 0)),
        ],
        out_specs=pl.BlockSpec((1, rows, width), lambda i: (i, 0, 0)),
        out_shape=jax.ShapeDtypeStruct((chips, rows, width), LOW),
        compiler_params=params(),
        cost_estimate=FREE,
    )(core, preceded, qkv, rims)


def attend_back_kernel(core, preceded, qkv, rim, d_mixed, out, lent):
    flipped = core[0] > 0
    ready = preceded[pl.program_id(0)]
    width = d_mixed.shape[2]
    heads = width // HEAD
    half = heads // CORES
    factor = HEAD ** (-0.5)
    for head in range(heads):
        queries, keys, values = (
            qkv[0, :, part * width + head * HEAD : part * width + (head + 1) * HEAD]
            for part in range(3)
        )
        rim_keys = rim[0, :, head * HEAD : (head + 1) * HEAD]
        rim_values = rim[0, :, width + head * HEAD : width + (head + 1) * HEAD]
        there = (head + half) % heads
        upstream = jnp.where(
            flipped,
            d_mixed[0, :, there * HEAD : (there + 1) * HEAD],
            d_mixed[0, :, head * HEAD : (head + 1) * HEAD],
        )
        steps = queries.shape[0] // BLOCK
        d_queries, d_keys, d_values = [], [], []
        for step in range(steps):
            rows = slice(step * BLOCK, (step + 1) * BLOCK)
            near_keys, near_values = windows(keys, rim_keys, step), windows(values, rim_values, step)
            probs = window_probs(queries[rows], near_keys, step == 0, ready)
            d_probs = matmul_cols(upstream[rows], near_values)
            d_scores = probs * (d_probs - jnp.sum(probs * d_probs, axis=-1, keepdims=True))
            d_scores = d_scores.astype(LOW)
            d_queries.append(matmul(d_scores, near_keys) * factor)
            d_keys.append(matmul_rows(d_scores, queries[rows]) * factor)
            d_values.append(matmul_rows(probs.astype(LOW), upstream[rows]))
        out[0, :, head * HEAD : (head + 1) * HEAD] = jnp.concatenate(d_queries, axis=0).astype(LOW)
        for part, grads in ((1, d_keys), (2, d_values)):
            first = (part - 1) * width + head * HEAD
            lent[0, :, first : first + HEAD] = grads[0][:WINDOW].astype(LOW)
            for step in range(steps):
                own = grads[step][WINDOW:]
                if step + 1 < steps:
                    keep = own[: BLOCK - WINDOW]
                    own = jnp.concatenate(
                        [keep, own[BLOCK - WINDOW :] + grads[step + 1][:WINDOW]], axis=0
                    )
                out[
                    0,
                    step * BLOCK : (step + 1) * BLOCK,
                    part * width + head * HEAD : part * width + (head + 1) * HEAD,
                ] = own.astype(LOW)


def attention_back(core, preceded, qkv, rims, d_mixed):
    chips, rows, columns = qkv.shape
    width = columns // 3
    return pl.pallas_call(
        attend_back_kernel,
        grid=(chips,),
        in_specs=[
            SCALAR,
            SCALAR,
            pl.BlockSpec((1, rows, columns), lambda i: (i, 0, 0)),
            pl.BlockSpec((1,) + rims.shape[1:], lambda i: (i, 0, 0)),
            pl.BlockSpec((1, rows, width), lambda i: (i, 0, 0)),
        ],
        out_specs=[
            pl.BlockSpec((1, rows, columns), lambda i: (i, 0, 0)),
            pl.BlockSpec((1,) + rims.shape[1:], lambda i: (i, 0, 0)),
        ],
        out_shape=[
            jax.ShapeDtypeStruct(qkv.shape, LOW),
            jax.ShapeDtypeStruct(rims.shape, LOW),
        ],
        compiler_params=params(),
        cost_estimate=FREE,
    )(core, preceded, qkv, rims, d_mixed)


def out_kernel(chips, core, mixed, mine, other, tokens, gain, resid, act):
    step, steps = pl.program_id(0), pl.num_programs(0)
    flipped = core[0] > 0

    @pl.when(step == 0)
    def _():
        resid[...] = tokens[...].astype(F32)

    @pl.when(step < steps // 2)
    def _():
        resid[...] += matmul(mixed[...], mine[...])

    @pl.when(step >= steps // 2)
    def _():
        resid[...] += matmul(mixed[...], other[...])

    @pl.when(step == steps - 1)
    def _():
        @pl.loop(0, tokens.shape[0], step=ROWS)
        def _(start):
            rows = pl.ds(pl.multiple_of(start, ROWS), ROWS)
            values = resid[rows, :]
            inverse = lax.rsqrt(jnp.mean(values * values, axis=-1, keepdims=True) + EPS)
            normed = own_columns(values * inverse, flipped, chips)
            act[rows, :] = (normed * gain[...]).astype(LOW)


def out_project(core, mixed, mine, other, tokens, gain, chips):
    rows, features = tokens.shape
    depth = mine.shape[0] // chips
    return pl.pallas_call(
        functools.partial(out_kernel, chips),
        grid=(2 * chips,),
        in_specs=[
            SCALAR,
            pl.BlockSpec((rows, depth), lambda i: (0, i)),
            pl.BlockSpec((depth, features), lambda i: (jnp.minimum(i, chips - 1), 0)),
            pl.BlockSpec((depth, features), lambda i: (jnp.maximum(i - chips, 0), 0)),
            whole(tokens.shape),
            whole(gain.shape),
        ],
        out_specs=[whole(tokens.shape), whole(tokens.shape)],
        out_shape=[
            jax.ShapeDtypeStruct(tokens.shape, F32),
            jax.ShapeDtypeStruct(tokens.shape, LOW),
        ],
        compiler_params=params(),
        cost_estimate=FREE,
    )(core, mixed, mine, other, tokens, gain)


def row_specs(steps, wholes, pairs, features):
    half = steps // 2

    def spec(first, last, count):
        low = functools.partial(lambda first, last, i: jnp.clip(i - first, 0, last - 1), first, last)
        if count == 2:
            return pl.BlockSpec((ROWS, features), lambda i: (low(i), 0))
        return pl.BlockSpec((None, ROWS, features), lambda i: (0, low(i), 0))

    specs = [spec(0, steps, 2) for _ in wholes]
    for first, second in pairs:
        specs += [spec(0, half, first.ndim), spec(half, half, second.ndim)]
    return specs


def sum_rows(step, steps, count, refs):
    total = sum(ref[...].astype(F32) for ref in refs[:count])
    for i in range(count, len(refs), 2):
        part = jnp.where(step < steps // 2, refs[i][...], refs[i + 1][...])
        total = total + part.astype(F32)
    return total


def norm_back_rows(chips, flipped, d_act, values, gain, upstream):
    d_act = natural_columns(d_act, flipped, chips)
    inverse = lax.rsqrt(jnp.mean(values * values, axis=-1, keepdims=True) + EPS)
    normed = values * inverse
    scaled = d_act * natural_columns(gain, flipped, chips)
    result = upstream + inverse * (
        scaled - normed * jnp.mean(scaled * normed, axis=-1, keepdims=True)
    )
    return result, jnp.sum(d_act * normed, axis=0, keepdims=True)


def middle_kernel(chips, steps, count, size, core, *refs):
    parts, refs = refs[:size], refs[size:]
    resid, gain, d_final, mine, other, d_resid, d_attn, d_mixed, gain_part = refs
    step = pl.program_id(0)
    flipped = core[0] > 0
    tall = resid.shape[0]

    @pl.when(step < steps)
    def _():
        grad, part = norm_back_rows(
            chips,
            flipped,
            sum_rows(step, steps, count, parts),
            resid[...],
            gain[...],
            d_final[...],
        )
        d_resid[...] = grad
        d_attn[pl.ds(pl.multiple_of(step * tall, tall), tall), :] = grad.astype(LOW)

        @pl.when(step == 0)
        def _():
            gain_part[...] = part

        @pl.when(step > 0)
        def _():
            gain_part[...] += part

    @pl.when(step == steps)
    def _():
        gain_part[...] = own_columns(gain_part[...], flipped, chips)

    @pl.when((step >= steps) & (step < steps + chips))
    def _():
        d_mixed[0] = matmul_cols(d_attn[...], mine[...]).astype(LOW)

    @pl.when(step >= steps + chips)
    def _():
        d_mixed[0] = matmul_cols(d_attn[...], other[...]).astype(LOW)


def middle(core, wholes, pairs, resid, gain, d_final, mine, other, chips):
    parts = list(wholes) + [half for pair in pairs for half in pair]
    rows, features = resid.shape
    steps = rows // ROWS
    depth = mine.shape[0] // chips

    def by_rows():
        return pl.BlockSpec((ROWS, features), lambda i: (jnp.minimum(i, steps - 1), 0))

    return pl.pallas_call(
        functools.partial(middle_kernel, chips, steps, len(wholes), len(parts)),
        grid=(steps + 2 * chips,),
        in_specs=[SCALAR]
        + row_specs(steps, wholes, pairs, features)
        + [
            by_rows(),
            whole(gain.shape),
            by_rows(),
            pl.BlockSpec((depth, features), lambda i: (jnp.clip(i - steps, 0, chips - 1), 0)),
            pl.BlockSpec(
                (depth, features), lambda i: (jnp.clip(i - steps - chips, 0, chips - 1), 0)
            ),
        ],
        out_specs=[
            by_rows(),
            whole(resid.shape),
            pl.BlockSpec(
                (1, rows, depth),
                lambda i: (
                    lax.rem(jnp.maximum(i - steps, 0), chips),
                    0,
                    lax.div(jnp.maximum(i - steps, 0), chips),
                ),
            ),
            whole((1, features)),
        ],
        out_shape=[
            jax.ShapeDtypeStruct(resid.shape, F32),
            jax.ShapeDtypeStruct(resid.shape, LOW),
            jax.ShapeDtypeStruct((chips, rows, 2 * depth), LOW),
            jax.ShapeDtypeStruct((1, features), F32),
        ],
        compiler_params=params(),
        cost_estimate=FREE,
    )(core, *parts, resid, gain, d_final, mine, other)


def last_kernel(chips, steps, count, core, *refs):
    parts, refs = refs[:-4], refs[-4:]
    tokens, gain, d_resid, out = refs
    out[...], _ = norm_back_rows(
        chips,
        core[0] > 0,
        sum_rows(pl.program_id(0), steps, count, parts),
        tokens[...].astype(F32),
        gain[...],
        d_resid[...],
    )


def last(core, wholes, pairs, tokens, gain, d_resid, chips):
    parts = list(wholes) + [half for pair in pairs for half in pair]
    rows, features = tokens.shape
    steps = rows // ROWS
    by_rows = pl.BlockSpec((ROWS, features), lambda i: (i, 0))
    return pl.pallas_call(
        functools.partial(last_kernel, chips, steps, len(wholes)),
        grid=(steps,),
        in_specs=[SCALAR]
        + row_specs(steps, wholes, pairs, features)
        + [by_rows, whole(gain.shape), by_rows],
        out_specs=by_rows,
        out_shape=jax.ShapeDtypeStruct(tokens.shape, F32),
        compiler_params=params(),
        cost_estimate=FREE,
    )(core, *parts, tokens, gain, d_resid)


def inner_first_kernel(act, gate, upward, out):
    out[...] = matmul(act[...], jnp.concatenate([gate[...], upward[...]], axis=1)).astype(LOW)


def inner_second_kernel(act, gate, upward, first, hidden, slope_gate, slope_up):
    width = gate.shape[1]
    both = first[...].astype(F32) + matmul(act[...], jnp.concatenate([gate[...], upward[...]], axis=1))
    gate, upward = both[:, :width], both[:, width:]
    sigma = jax.nn.sigmoid(gate)
    silu = gate * sigma
    hidden[...] = (silu * upward).astype(LOW)
    slope_gate[...] = (upward * sigma * (1.0 + gate * (1.0 - sigma))).astype(LOW)
    slope_up[...] = silu.astype(LOW)


def inner_specs(act, weights, part):
    rows = act.shape[0]
    half, columns = weights.shape
    tiles = columns // (2 * LANES)
    return tiles, [
        pl.BlockSpec((rows, half), lambda i: (0, part)),
        pl.BlockSpec((half, LANES), lambda i: (0, i)),
        pl.BlockSpec((half, LANES), lambda i: (0, tiles + i)),
    ]


def inner_first(act, weights):
    rows, columns = act.shape[0], weights.shape[1]
    if columns % (2 * LANES):
        return matmul(act[:, : weights.shape[0]], weights).astype(LOW)
    tiles, specs = inner_specs(act, weights, 0)
    return pl.pallas_call(
        inner_first_kernel,
        grid=(tiles,),
        in_specs=specs,
        out_specs=pl.BlockSpec((rows, 2 * LANES), lambda i: (0, i)),
        out_shape=jax.ShapeDtypeStruct((rows, columns), LOW),
        compiler_params=params(),
        cost_estimate=FREE,
    )(act, weights, weights)


def inner_second(act, weights, first):
    rows, columns = act.shape[0], weights.shape[1]
    width = columns // 2
    if columns % (2 * LANES):
        both = first.astype(F32) + matmul(act[:, weights.shape[0] :], weights)
        gate, upward = both[:, :width], both[:, width:]
        sigma = jax.nn.sigmoid(gate)
        silu = gate * sigma
        slope = upward * sigma * (1.0 + gate * (1.0 - sigma))
        return (silu * upward).astype(LOW), slope.astype(LOW), silu.astype(LOW)
    tiles, specs = inner_specs(act, weights, 1)
    tile = pl.BlockSpec((rows, LANES), lambda i: (0, i))
    return pl.pallas_call(
        inner_second_kernel,
        grid=(tiles,),
        in_specs=specs + [pl.BlockSpec((rows, 2 * LANES), lambda i: (0, i))],
        out_specs=[tile] * 3,
        out_shape=[jax.ShapeDtypeStruct((rows, width), LOW)] * 3,
        compiler_params=params(),
        cost_estimate=FREE,
    )(act, weights, weights, first)


def place_halves(flag, mine, other, out):
    rows = mine.shape[0]
    core = flag[0]
    out[pl.ds(pl.multiple_of(core * rows, 16), rows), :] = mine[...]
    out[pl.ds(pl.multiple_of((1 - core) * rows, 16), rows), :] = other[...]


def inner_back_kernel(flag, d_ffn, mine, other, slope_gate, slope_up, out, down):
    @pl.when(pl.program_id(0) == 0)
    def _():
        place_halves(flag, mine, other, down)

    width = down.shape[0]
    d_hidden = matmul_cols(d_ffn[...], down[...])
    out[:, :width] = (d_hidden * slope_gate[...]).astype(LOW)
    out[:, width:] = (d_hidden * slope_up[...]).astype(LOW)


def inner_back(flag, d_ffn, mine, other, slope_gate, slope_up, chips):
    rows, features = d_ffn.shape
    width = 2 * mine.shape[0]
    if width % LANES:
        d_hidden = matmul_cols(d_ffn, core_rows(mine, other))
        return jnp.concatenate([d_hidden * slope_gate, d_hidden * slope_up], axis=1).astype(LOW)
    tall = rows // chips
    flat = pl.BlockSpec((tall, width), lambda i: (i, 0))
    return pl.pallas_call(
        inner_back_kernel,
        grid=(chips,),
        in_specs=[
            SCALAR,
            pl.BlockSpec((tall, features), lambda i: (i, 0)),
            whole(mine.shape),
            whole(other.shape),
            flat,
            flat,
        ],
        out_specs=pl.BlockSpec((tall, 2 * width), lambda i: (i, 0)),
        out_shape=jax.ShapeDtypeStruct((rows, 2 * width), LOW),
        scratch_shapes=[pltpu.VMEM((width, features), LOW)],
        compiler_params=params(60),
        cost_estimate=FREE,
    )(flag, d_ffn, mine, other, slope_gate, slope_up)


def back_project_kernel(tiles, chips, d_out, mine, other, *refs):
    act, outs, total = (refs[0], refs[1:-1], refs[-1]) if chips == 0 else (None, refs, None)
    step = pl.program_id(0)
    columns = d_out.shape[1]

    def work(weights):
        grad = matmul_cols(d_out[...], weights[:, :columns])
        if act is not None:
            total[...] = jnp.sum(grad * act[...].astype(F32), axis=0, keepdims=True)
        spread(grad.astype(LOW), outs)

    @pl.when(step < tiles)
    def _():
        work(mine)

    @pl.when(step >= tiles)
    def _():
        work(other)


def back_project(d_out, mine, other, chips, *act):
    rows, columns = d_out.shape
    half = mine.shape[0]
    tile = 2 * LANES
    tiles = half // tile
    shapes = spread_shapes(chips, rows, 2 * half)
    flat = pl.BlockSpec((rows, tile), lambda i: (0, i))
    outs = pl.pallas_call(
        functools.partial(back_project_kernel, tiles, 0 if act else 1),
        grid=(2 * tiles,),
        in_specs=[
            whole(d_out.shape),
            pl.BlockSpec((tile, mine.shape[1]), lambda i: (jnp.minimum(i, tiles - 1), 0)),
            pl.BlockSpec((tile, mine.shape[1]), lambda i: (jnp.maximum(i - tiles, 0), 0)),
        ]
        + [flat for _ in act],
        out_specs=[column_spec(shape, tile) for shape in shapes]
        + [pl.BlockSpec((1, tile), lambda i: (0, i)) for _ in act],
        out_shape=[jax.ShapeDtypeStruct(shape, LOW) for shape in shapes]
        + [jax.ShapeDtypeStruct((1, 2 * half), F32) for _ in act],
        compiler_params=params(40),
        cost_estimate=FREE,
    )(d_out, mine, other, *act)
    return (outs[:-1], outs[-1]) if act else outs


def turned_kernel(count, left, right, *refs):
    arrived, outs = refs[:count], refs[count:]
    total = matmul_rows(left[...], right[...])
    if arrived:
        total = total + arrived[0][...].astype(F32)
    spread(total.astype(LOW), outs)


def turned(left, part, right, *arrived, chips=1):
    rows, half = left.shape[0], left.shape[1] // CORES
    width = right.shape[1]
    tile = LANES if width % (2 * LANES) else 2 * LANES
    shapes = spread_shapes(chips, half, width)
    outs = pl.pallas_call(
        functools.partial(turned_kernel, len(arrived)),
        grid=(width // tile,),
        in_specs=[
            pl.BlockSpec((rows, half), lambda i: (0, part)),
            pl.BlockSpec((rows, tile), lambda i: (0, i)),
        ]
        + [pl.BlockSpec((half, tile), lambda i: (0, i)) for _ in arrived],
        out_specs=[column_spec(shape, tile) for shape in shapes],
        out_shape=[jax.ShapeDtypeStruct(shape, LOW) for shape in shapes],
        compiler_params=params(60 if width > half * 2 else 32),
        cost_estimate=FREE,
    )(left, right, *arrived)
    return outs[0] if chips == 1 else outs


def inner_out_kernel(flag, left, mine, other, *refs):
    outs, down = refs[:-1], refs[-1]
    step = pl.program_id(0)

    @pl.when(step == 0)
    def _():
        place_halves(flag, mine, other, down)

    spread_step(step, matmul(left[...], down[...]).astype(LOW), outs)


def inner_out(flag, hidden, mine, other, chips):
    rows, width = hidden.shape
    features = mine.shape[1]
    if width % LANES:
        return [matmul(hidden, core_rows(mine, other)).astype(LOW)]
    tall = rows // chips
    shapes = spread_shapes(chips, rows, features)
    flat = pl.BlockSpec((tall, features), lambda i: (i, 0))
    return pl.pallas_call(
        inner_out_kernel,
        grid=(chips,),
        in_specs=[
            SCALAR,
            pl.BlockSpec((tall, width), lambda i: (i, 0)),
            whole(mine.shape),
            whole(other.shape),
        ],
        out_specs=[flat] if len(shapes) == 1 else [whole(shape) for shape in shapes],
        out_shape=[jax.ShapeDtypeStruct(shape, LOW) for shape in shapes],
        scratch_shapes=[pltpu.VMEM((width, features), LOW)],
        compiler_params=params(36),
        cost_estimate=FREE,
    )(flag, hidden, mine, other)


def half_kernel(flag, left, right, *refs):
    arrived, out = refs[:-1], refs[-1]
    rows = out.shape[0]
    start = left.shape[1] - rows
    wide = -(-rows // LANES) * LANES
    second = flag[0] > 0
    first = pl.multiple_of(jnp.where(second, left.shape[1] - wide, 0), LANES)
    total = matmul_rows(left[:, pl.ds(first, wide)], right[...])
    total = jnp.where(second, total[wide - rows :], total[:rows])
    if arrived:
        total = total + arrived[0][...].astype(F32)
    out[...] = total.astype(LOW)


def half_product(flag, left, right, *arrived):
    rows, columns = left.shape
    width = right.shape[1]
    half = columns // 2
    if columns % LANES:
        total = matmul_rows(left, right)
        total = jnp.where(flag[0] > 0, total[half:], total[:half])
        return sum([part.astype(F32) for part in arrived], total).astype(LOW)
    tile = 2 * LANES
    return pl.pallas_call(
        half_kernel,
        grid=(width // tile,),
        in_specs=[SCALAR, whole(left.shape), pl.BlockSpec((rows, tile), lambda i: (0, i))]
        + [pl.BlockSpec((half, tile), lambda i: (0, i)) for _ in arrived],
        out_specs=pl.BlockSpec((half, tile), lambda i: (0, i)),
        out_shape=jax.ShapeDtypeStruct((half, width), LOW),
        compiler_params=params(60),
        cost_estimate=FREE,
    )(flag, left, right, *arrived)


def per_device(
    tokens,
    out_cotangent,
    group_ids,
    attn_gain,
    query_weight,
    key_weight,
    value_weight,
    out_weight,
    ffn_gain,
    gate_weight,
    up_weight,
    down_weight,
):
    tok_count, features = tokens.shape[1:]
    weight_rows, inner = gate_weight.shape
    chips = chip_count()
    chip, core = own_chip(), own_core()
    ids = lax.iota(jnp.int32, chips)
    head_width, inner_width = features // chips, inner // chips
    half = features // CORES
    flag = jnp.full((1,), core, jnp.int32)
    tokens, out_cotangent = tokens[0], out_cotangent[0]

    gains = jnp.concatenate(
        [
            jnp.broadcast_to(attn_gain[:, None], (weight_rows, LANES // 2)),
            jnp.broadcast_to(ffn_gain[:, None], (weight_rows, LANES // 2)),
        ],
        axis=1,
    )

    def for_chip(weight, k):
        width = weight.shape[1] // chips
        return lax.dynamic_slice_in_dim(weight, (chip ^ k) * width, width, axis=1)

    def rows_of_chips(weights, *others):
        parts = [jnp.concatenate([for_chip(w, k) for w in weights], axis=1) for k in range(chips)]
        parts = [jnp.concatenate([part] + list(others), axis=1) for part in parts]
        return jnp.stack(in_order(chips_scatter(parts)))

    group_span = GPS * lax.axis_size("batch")
    onehot = (group_ids[0, :, None] == jnp.arange(group_span, dtype=jnp.int32)[None, :]).astype(F32)
    group_total = seq_sum(jnp.sum(onehot, axis=0, keepdims=True))
    own_total = jnp.sum(onehot * group_total, axis=-1)[:, None]
    weighting = tok_count * lax.axis_size("seq") / (GPS * own_total)
    d_final = out_cotangent.astype(F32) * weighting

    out_mine = batch_gather(out_weight, 0)
    qkv_rows = rows_of_chips([query_weight, key_weight, value_weight], gains)
    qkv_mine = batch_gather(after(qkv_rows, out_mine), 1).reshape(half, -1)
    tokens_sent = after(tokens, qkv_rows, group_total)
    tokens_near = [exchange(tokens_sent, CORES * k) for k in range(1, chips)]
    gathered = gathered_rows(tokens_sent, tokens_near, [])
    gate_weight, up_weight = after((gate_weight, up_weight), gathered)
    inner_rows = rows_of_chips([gate_weight, up_weight])
    inner_mine = batch_gather(inner_rows, 1).reshape(half, -1)
    down_mine = batch_gather(after(down_weight, inner_rows), 0)

    ffn_sent = after(d_final.astype(LOW), inner_rows)
    ffn_near = gather_near(ffn_sent)
    qkv_mine = after(qkv_mine, *ffn_near)
    ffn_far = gather_far(ffn_near)
    out_sent = after(out_mine, *ffn_near)
    out_near = gather_near(out_sent)
    qkv_other = swap_core(qkv_mine)
    out_far = gather_far(out_near)
    columns = 3 * head_width
    gain_one, gain_two = (
        jnp.concatenate([qkv_mine[:, place], qkv_other[:, place]]).astype(F32)[None]
        for place in (columns, columns + LANES // 2)
    )
    act_one, qkv = project(flag, gathered, gain_one, qkv_mine, qkv_other, columns, chips)
    qkv = qkv.reshape(chips, tok_count, columns)
    place = chip ^ ids
    tails = swap_core(qkv[:, tok_count - WINDOW :, head_width:])
    before = jnp.where(core > 0, ids, chip ^ jnp.maximum(place - 1, 0))
    follow = jnp.where(core > 0, chip ^ jnp.minimum(place + 1, chips - 1), ids)
    preceded = ((core > 0) | (place > 0)).astype(jnp.int32)
    followed = (core == 0) | (place < chips - 1)
    rims = jnp.take(after(tails, *out_near), before, axis=0)
    mixed = attention(flag, preceded, qkv, rims)

    mixed = after(mixed, *out_far, *ffn_far)
    mixed_own = chips_scatter([mixed[k] for k in range(chips)])
    cell = head_width // CORES
    mixed_own = jnp.concatenate(
        [block[:, i * cell : (i + 1) * cell] for i in range(CORES) for block in mixed_own], axis=1
    )
    out_near = after(out_near, mixed)
    out_half = gathered_rows(out_sent, out_near, out_far)
    out_other = swap_core(out_half)
    resid, act_two_own = out_project(
        flag, mixed_own, out_half, out_other, tokens, gain_two, chips
    )

    d_ffn = gathered_rows(ffn_sent, ffn_near, ffn_far)
    act_two_own = after(act_two_own, d_ffn)
    act_near = gather_near(act_two_own)
    act_far = gather_far(after(act_near, inner_mine))
    act_two = gathered_rows(act_two_own, act_near, act_far)
    inner_mine = after(inner_mine, *act_near)
    inner_other = swap_core(inner_mine)
    hidden, slope_gate, slope_up = inner_second(
        act_two, inner_other, inner_first(act_two, inner_mine)
    )
    down_send = half_product(1 - flag, hidden, d_ffn)
    down_back = swap_core(down_send)
    down_mine = after(down_mine, down_send)
    down_sum = half_product(flag, hidden, after(d_ffn, down_send, down_mine), down_back)
    down_other = swap_core(down_mine)
    down_grad = batch_scatter(down_sum, 0)
    d_gate_up = inner_back(
        flag, after(d_ffn, down_sum), down_mine, down_other, slope_gate, slope_up, chips
    )
    inner_send = turned(act_two, 1, d_gate_up)
    act_parts = back_project(after(d_gate_up, inner_send), inner_mine, inner_other, chips)
    act_near = chips_sum_near(act_parts)
    inner_sum = turned(
        act_two, 0, after(d_gate_up, act_parts[0], down_grad), swap_core(inner_send)
    )
    act_far = chips_sum_far(act_parts, act_near)
    inner_sum = after(inner_sum, *act_near)
    inner_grad = batch_scatter(inner_sum.reshape(chips, half // chips, -1), 1)
    d_resid, d_attn, d_mixed_own, gain_two_part = middle(
        flag,
        *summands(act_parts, act_near, act_far),
        resid,
        gain_two,
        d_final,
        out_half,
        out_other,
        chips,
    )

    d_mixed_parts = chips_scatter([d_mixed_own[k] for k in range(chips)])
    d_mixed = jnp.stack(d_mixed_parts)
    d_qkv, lent = attention_back(flag, preceded, qkv, rims, d_mixed)
    lent = swap_core(lent)
    block_parts = inner_out(flag, after(hidden, d_mixed_own), down_mine, down_other, chips)
    block_near = chips_sum_near(block_parts)

    returned = jnp.where(followed[:, None, None], jnp.take(lent, follow, axis=0), 0)
    d_qkv = d_qkv.at[:, tok_count - WINDOW :, head_width:].add(returned)
    d_qkv = after(d_qkv.reshape(chips * tok_count, columns), *block_near)
    block_far = chips_sum_far(block_parts, block_near)
    qkv_send = turned(act_one, 1, d_qkv)
    out_send = turned(mixed_own, 1, after(d_attn, qkv_send))
    d_act_parts, gain_one_part = back_project(
        after(d_qkv, out_send), qkv_mine, qkv_other, chips, act_one
    )
    qkv_sum = turned(act_one, 0, after(d_qkv, d_act_parts[0]), swap_core(qkv_send))
    out_parts = turned(mixed_own, 0, after(d_attn, qkv_sum), swap_core(out_send), chips=chips)
    if chips == 1:
        out_parts = [out_parts]
    d_act_near = after(chips_sum_near(d_act_parts), out_parts[0])
    out_parts = after(out_parts, *d_act_near)
    out_near = chips_sum_near(out_parts)
    qkv_sum = after(qkv_sum, inner_grad)
    qkv_grad = batch_scatter(qkv_sum.reshape(chips, half // chips, -1), 1)
    out_far = chips_sum_far(out_parts, out_near)
    d_act_near = after(d_act_near, qkv_grad, *out_far)
    d_act_far = chips_sum_far(d_act_parts, d_act_near)
    gain_parts = jnp.concatenate([gain_one_part / gain_one, gain_two_part], axis=0)
    gain_parts = after(gain_parts, *d_act_far)
    gain_grads = gain_parts[:, :half] + swap_core(gain_parts[:, half:])
    gain_grads = gain_grads.reshape(2, chips, -1)
    gain_grads = [
        lax.dynamic_index_in_dim(gain_grads, chip ^ k, axis=1, keepdims=False)
        for k in range(chips)
    ]
    gain_grads = sum(chips_scatter(gain_grads)).reshape(2, lax.axis_size("batch"), -1)
    row = lax.axis_index("batch")
    gain_grads = sum(
        exchange(
            lax.dynamic_index_in_dim(gain_grads, row ^ k, axis=1, keepdims=False), k, "batch"
        )
        for k in range(lax.axis_size("batch"))
    )
    out_sum = summed(out_parts, out_near, out_far).astype(LOW)
    out_grad = batch_scatter(after(out_sum, qkv_grad), 0)
    tokens_grad = last(
        flag, *summands(d_act_parts, d_act_near, d_act_far), tokens, gain_one, d_resid, chips
    )
    block_out = (resid + summed(block_parts, block_near, block_far)).astype(LOW)

    def columns_of_chips(grad):
        chip_rows = [
            lax.dynamic_index_in_dim(grad, chip ^ k, axis=0, keepdims=False) for k in range(chips)
        ]
        return in_order(chips_scatter(chip_rows))

    inner_grad = columns_of_chips(inner_grad)
    qkv_grad = columns_of_chips(after(qkv_grad, *d_act_far))

    def whole_columns(blocks, first, width):
        parts = [block[:, first : first + width] for block in blocks]
        return jnp.concatenate(parts, axis=1).astype(F32)


    return (
        block_out[None],
        tokens_grad[None],
        gain_grads[0],
        whole_columns(qkv_grad, 0, head_width),
        whole_columns(qkv_grad, head_width, head_width),
        whole_columns(qkv_grad, 2 * head_width, head_width),
        out_grad.astype(F32),
        gain_grads[1],
        whole_columns(inner_grad, 0, inner_width),
        whole_columns(inner_grad, inner_width, inner_width),
        down_grad.astype(F32),
    )


def solution(mesh):
    rows = P(("seq", "batch"), None)
    vector = P(("seq", "batch"))
    cells = P("batch", "seq", None)
    return jax.shard_map(
        per_device,
        mesh=mesh,
        in_specs=(cells, cells, P("batch", "seq"))
        + (vector, rows, rows, rows, rows, vector, rows, rows, rows),
        out_specs=(cells, cells, vector, rows, rows, rows, rows, vector, rows, rows, rows),
        check_vma=False,
    )
```

```python
import functools

import jax
import jax.numpy as jnp
from jax import lax
from jax.experimental import pallas as pl
from jax.experimental.pallas import tpu as pltpu
from jax.sharding import PartitionSpec as P

HEAD = 128
WINDOW = 64
GPS = 4
CORES = 2

EPS = 1e-05
NEGATIVE = -1e30
ROWS_DIMS = (((0,), (0,)), ((), ()))
COLS_DIMS = (((1,), (1,)), ((), ()))
BLOCK = 128
ROWS = 64
LANES = 128
F32 = jnp.float32
LOW = jnp.bfloat16


def matmul(left, right):
    return jnp.dot(left, right, preferred_element_type=F32)


def matmul_rows(left, right):
    return lax.dot_general(left, right, ROWS_DIMS, preferred_element_type=F32)


def matmul_cols(left, right):
    return lax.dot_general(left, right, COLS_DIMS, preferred_element_type=F32)


def exchange(value, flip, axis="seq"):
    if flip == 0:
        return value
    count = lax.axis_size(axis)
    return lax.ppermute(value, axis, [(place, place ^ flip) for place in range(count)])


def swap_core(value):
    return exchange(value, 1)


def chip_count():
    return lax.axis_size("seq") // CORES


def own_chip():
    return lax.axis_index("seq") // CORES


def own_core():
    return lax.axis_index("seq") % CORES


def gather_near(value):
    if chip_count() != 4:
        return [exchange(value, CORES * k) for k in range(1, chip_count())]
    return [exchange(value, CORES), exchange(value, 2 * CORES)]


def gather_far(near):
    if chip_count() != 4:
        return []
    half = near[0].shape[0] // 2
    return [exchange(near[0][:half], 2 * CORES), exchange(near[1][half:], CORES)]


def gathered_rows(value, near, far):
    return jnp.concatenate([value] + near + far, axis=0)


def chips_scatter(blocks):
    return [blocks[0]] + [exchange(blocks[k], CORES * k) for k in range(1, chip_count())]


def chips_sum_near(parts):
    if chip_count() != 4:
        blocks = parts[0].reshape((chip_count(), -1) + parts[0].shape[1:])
        return chips_scatter([blocks[k] for k in range(chip_count())])
    return [exchange(parts[1], CORES), exchange(parts[2], 2 * CORES)]


def chips_sum_between(parts, near):
    if chip_count() != 4:
        return []
    on_second = (parts[3].astype(F32) + near[0][1].astype(F32)).astype(LOW)
    on_first = (parts[4].astype(F32) + near[1][1].astype(F32)).astype(LOW)
    return [on_second, on_first]


def chips_sum_far(parts, near):
    return chips_sum_send(chips_sum_between(parts, near))


def chips_sum_send(between):
    return [exchange(part, step * CORES) for part, step in zip(between, (2, 1))]


def summands(parts, near, far):
    if not far:
        return near, []
    return [parts[0]], [(near[0][0], near[1][0]), tuple(far)]


def summed(parts, near, far):
    wholes, pairs = summands(parts, near, far)
    total = sum(part.astype(F32) for part in wholes)
    return total + sum(jnp.concatenate(pair, axis=0).astype(F32) for pair in pairs)


def spread_shapes(chips, rows, columns):
    if chips != 4:
        return [(rows, columns)]
    tall, low = rows // chips, rows // chips // 2
    return [(tall, columns), (2, low, columns), (2, low, columns), (low, columns), (low, columns)]


def spread_block(block, value, outs, place=slice(None)):
    own, first, second, keep_second, keep_first = outs
    low = value.shape[0] // 2
    if block == 0:
        own[:, place] = value
    if block == 1:
        first[0, :, place] = value[:low]
        keep_first[:, place] = value[low:]
    if block == 2:
        keep_second[:, place] = value[:low]
        second[0, :, place] = value[low:]
    if block == 3:
        first[1, :, place] = value[:low]
        second[1, :, place] = value[low:]


def spread(total, outs):
    if len(outs) == 1:
        outs[0][...] = total
        return
    tall = total.shape[0] // 4
    for block in range(4):
        spread_block(block, total[block * tall : (block + 1) * tall], outs)


def column_spec(shape, tile):
    lead = (0,) * (len(shape) - 1)
    return pl.BlockSpec(shape[:-1] + (tile,), lambda i: lead + (i,))


def spread_step(step, value, outs, place=slice(None)):
    if len(outs) == 1:
        outs[0][:, place] = value
        return
    for block in range(4):

        @pl.when(step == block)
        def _():
            spread_block(block, value, outs, place)


def in_order(blocks):
    chip = own_chip()
    bit = 1
    while bit < len(blocks):
        flipped = (chip & bit) > 0
        blocks = [jnp.where(flipped, blocks[i ^ bit], blocks[i]) for i in range(len(blocks))]
        bit *= 2
    return blocks


def to_chips(value):
    chip = own_chip()
    blocks = [
        lax.dynamic_index_in_dim(value, chip ^ k, axis=0, keepdims=False)
        for k in range(chip_count())
    ]
    return jnp.stack(in_order(chips_scatter(blocks)))


def after(value, *others):
    return lax.optimization_barrier((value,) + others)[0]


def seq_sum(value):
    bit = 1
    while bit < lax.axis_size("seq"):
        value = value + exchange(value, bit)
        bit *= 2
    return value


def own_first(first, second):
    flipped = own_core() > 0
    return jnp.where(flipped, second, first), jnp.where(flipped, first, second)


def core_rows(mine, other):
    return jnp.concatenate(own_first(mine, other), axis=0)


def batch_gather(value, axis):
    return lax.all_gather(value, "batch", axis=axis, tiled=True)


def batch_scatter(value, axis):
    return lax.psum_scatter(value, "batch", scatter_dimension=axis, tiled=True)


FREE = pl.CostEstimate(flops=0, bytes_accessed=0, transcendentals=0)


def params(megabytes=32):
    return pltpu.CompilerParams(vmem_limit_bytes=megabytes * 2**20)


def whole(shape):
    return pl.BlockSpec(shape, lambda *step: (0,) * len(shape))


SCALAR = pl.BlockSpec(memory_space=pltpu.SMEM)


def own_columns(values, flipped, chips):
    width = values.shape[1] // (chips * CORES)
    cells = [values[:, i * width : (i + 1) * width] for i in range(chips * CORES)]
    mine = [jnp.where(flipped, cells[2 * q + 1], cells[2 * q]) for q in range(chips)]
    other = [jnp.where(flipped, cells[2 * q], cells[2 * q + 1]) for q in range(chips)]
    return jnp.concatenate(mine + other, axis=1)


def natural_columns(values, flipped, chips):
    width = values.shape[1] // (chips * CORES)
    cells = [values[:, i * width : (i + 1) * width] for i in range(chips * CORES)]
    pairs = []
    for q in range(chips):
        mine, other = cells[q], cells[chips + q]
        pairs += [jnp.where(flipped, other, mine), jnp.where(flipped, mine, other)]
    return jnp.concatenate(pairs, axis=1)


def project_kernel(chips, core, tokens, gain, mine, other, act, out):
    flipped = core[0] > 0
    half, columns = mine.shape[0], out.shape[1]

    @pl.loop(0, tokens.shape[0], step=ROWS)
    def _(start):
        rows = pl.ds(pl.multiple_of(start, ROWS), ROWS)
        values = tokens[rows, :].astype(F32)
        inverse = lax.rsqrt(jnp.mean(values * values, axis=-1, keepdims=True) + EPS)
        act[rows, :] = (own_columns(values * inverse, flipped, chips) * gain[...]).astype(LOW)

    total = matmul(act[:, :half], mine[:, :columns]) + matmul(act[:, half:], other[:, :columns])
    out[...] = total.astype(LOW)


def project(core, tokens, gain, mine, other, columns, chips):
    rows, features = tokens.shape
    tall = rows // chips
    return pl.pallas_call(
        functools.partial(project_kernel, chips),
        grid=(chips,),
        in_specs=[
            SCALAR,
            pl.BlockSpec((tall, features), lambda i: (i, 0)),
            whole(gain.shape),
            whole(mine.shape),
            whole(other.shape),
        ],
        out_specs=[
            pl.BlockSpec((tall, features), lambda i: (i, 0)),
            pl.BlockSpec((tall, columns), lambda i: (i, 0)),
        ],
        out_shape=[
            jax.ShapeDtypeStruct((rows, features), LOW),
            jax.ShapeDtypeStruct((rows, columns), LOW),
        ],
        compiler_params=params(40),
        cost_estimate=FREE,
    )(core, tokens, gain, mine, other)


def windows(keys, rim, step):
    if step == 0:
        return jnp.concatenate([rim, keys[:BLOCK]], axis=0)
    return keys[step * BLOCK - WINDOW : (step + 1) * BLOCK]


def window_probs(queries, keys, first, preceded):
    scores = matmul_cols(queries, keys) * HEAD ** (-0.5)
    query = lax.broadcasted_iota(jnp.int32, scores.shape, 0)
    key = lax.broadcasted_iota(jnp.int32, scores.shape, 1)
    allowed = (key > query) & (key <= query + WINDOW)
    if first:
        allowed = allowed & ((key >= WINDOW) | (preceded > 0))
    scores = jnp.where(allowed, scores, NEGATIVE)
    expo = jnp.exp(scores - jnp.max(scores, axis=-1, keepdims=True))
    return expo / jnp.sum(expo, axis=-1, keepdims=True)


def attend_kernel(core, preceded, qkv, rim, out):
    flipped = core[0] > 0
    ready = preceded[pl.program_id(0)]
    width = out.shape[2]
    heads = width // HEAD
    mixed = []
    for head in range(heads):
        cell = slice(head * HEAD, (head + 1) * HEAD)
        queries, keys, values = (
            qkv[0, :, part * width + head * HEAD : part * width + (head + 1) * HEAD]
            for part in range(3)
        )
        rim_keys = rim[0, :, cell]
        rim_values = rim[0, :, width + head * HEAD : width + (head + 1) * HEAD]
        rows = []
        for step in range(queries.shape[0] // BLOCK):
            probs = window_probs(
                queries[step * BLOCK : (step + 1) * BLOCK],
                windows(keys, rim_keys, step),
                step == 0,
                ready,
            )
            rows.append(matmul(probs.astype(LOW), windows(values, rim_values, step)))
        mixed.append(jnp.concatenate(rows, axis=0).astype(LOW))
    half = heads // CORES
    for head in range(half):
        first, second = mixed[head], mixed[half + head]
        out[0, :, head * HEAD : (head + 1) * HEAD] = jnp.where(flipped, second, first)
        out[0, :, (half + head) * HEAD : (half + head + 1) * HEAD] = jnp.where(
            flipped, first, second
        )


def attention(core, preceded, qkv, rims):
    chips, rows, columns = qkv.shape
    width = columns // 3
    return pl.pallas_call(
        attend_kernel,
        grid=(chips,),
        in_specs=[
            SCALAR,
            SCALAR,
            pl.BlockSpec((1, rows, columns), lambda i: (i, 0, 0)),
            pl.BlockSpec((1,) + rims.shape[1:], lambda i: (i, 0, 0)),
        ],
        out_specs=pl.BlockSpec((1, rows, width), lambda i: (i, 0, 0)),
        out_shape=jax.ShapeDtypeStruct((chips, rows, width), LOW),
        compiler_params=params(),
        cost_estimate=FREE,
    )(core, preceded, qkv, rims)


def attend_back_kernel(core, preceded, qkv, rim, d_mixed, out, lent):
    flipped = core[0] > 0
    ready = preceded[pl.program_id(0)]
    width = d_mixed.shape[2]
    heads = width // HEAD
    half = heads // CORES
    factor = HEAD ** (-0.5)
    for head in range(heads):
        queries, keys, values = (
            qkv[0, :, part * width + head * HEAD : part * width + (head + 1) * HEAD]
            for part in range(3)
        )
        rim_keys = rim[0, :, head * HEAD : (head + 1) * HEAD]
        rim_values = rim[0, :, width + head * HEAD : width + (head + 1) * HEAD]
        there = (head + half) % heads
        upstream = jnp.where(
            flipped,
            d_mixed[0, :, there * HEAD : (there + 1) * HEAD],
            d_mixed[0, :, head * HEAD : (head + 1) * HEAD],
        )
        steps = queries.shape[0] // BLOCK
        d_queries, d_keys, d_values = [], [], []
        for step in range(steps):
            rows = slice(step * BLOCK, (step + 1) * BLOCK)
            near_keys, near_values = windows(keys, rim_keys, step), windows(values, rim_values, step)
            probs = window_probs(queries[rows], near_keys, step == 0, ready)
            d_probs = matmul_cols(upstream[rows], near_values)
            d_scores = probs * (d_probs - jnp.sum(probs * d_probs, axis=-1, keepdims=True))
            d_scores = d_scores.astype(LOW)
            d_queries.append(matmul(d_scores, near_keys) * factor)
            d_keys.append(matmul_rows(d_scores, queries[rows]) * factor)
            d_values.append(matmul_rows(probs.astype(LOW), upstream[rows]))
        out[0, :, head * HEAD : (head + 1) * HEAD] = jnp.concatenate(d_queries, axis=0).astype(LOW)
        for part, grads in ((1, d_keys), (2, d_values)):
            first = (part - 1) * width + head * HEAD
            lent[0, :, first : first + HEAD] = grads[0][:WINDOW].astype(LOW)
            for step in range(steps):
                own = grads[step][WINDOW:]
                if step + 1 < steps:
                    keep = own[: BLOCK - WINDOW]
                    own = jnp.concatenate(
                        [keep, own[BLOCK - WINDOW :] + grads[step + 1][:WINDOW]], axis=0
                    )
                out[
                    0,
                    step * BLOCK : (step + 1) * BLOCK,
                    part * width + head * HEAD : part * width + (head + 1) * HEAD,
                ] = own.astype(LOW)


def attention_back(core, preceded, qkv, rims, d_mixed):
    chips, rows, columns = qkv.shape
    width = columns // 3
    return pl.pallas_call(
        attend_back_kernel,
        grid=(chips,),
        in_specs=[
            SCALAR,
            SCALAR,
            pl.BlockSpec((1, rows, columns), lambda i: (i, 0, 0)),
            pl.BlockSpec((1,) + rims.shape[1:], lambda i: (i, 0, 0)),
            pl.BlockSpec((1, rows, width), lambda i: (i, 0, 0)),
        ],
        out_specs=[
            pl.BlockSpec((1, rows, columns), lambda i: (i, 0, 0)),
            pl.BlockSpec((1,) + rims.shape[1:], lambda i: (i, 0, 0)),
        ],
        out_shape=[
            jax.ShapeDtypeStruct(qkv.shape, LOW),
            jax.ShapeDtypeStruct(rims.shape, LOW),
        ],
        compiler_params=params(),
        cost_estimate=FREE,
    )(core, preceded, qkv, rims, d_mixed)


def out_kernel(chips, core, mixed, mine, other, tokens, gain, resid, act):
    step, steps = pl.program_id(0), pl.num_programs(0)
    flipped = core[0] > 0

    @pl.when(step == 0)
    def _():
        resid[...] = tokens[...].astype(F32)

    @pl.when(step < steps // 2)
    def _():
        resid[...] += matmul(mixed[...], mine[...])

    @pl.when(step >= steps // 2)
    def _():
        resid[...] += matmul(mixed[...], other[...])

    @pl.when(step == steps - 1)
    def _():
        @pl.loop(0, tokens.shape[0], step=ROWS)
        def _(start):
            rows = pl.ds(pl.multiple_of(start, ROWS), ROWS)
            values = resid[rows, :]
            inverse = lax.rsqrt(jnp.mean(values * values, axis=-1, keepdims=True) + EPS)
            normed = own_columns(values * inverse, flipped, chips)
            act[rows, :] = (normed * gain[...]).astype(LOW)


def out_project(core, mixed, mine, other, tokens, gain, chips):
    rows, features = tokens.shape
    depth = mine.shape[0] // chips
    return pl.pallas_call(
        functools.partial(out_kernel, chips),
        grid=(2 * chips,),
        in_specs=[
            SCALAR,
            pl.BlockSpec((rows, depth), lambda i: (0, i)),
            pl.BlockSpec((depth, features), lambda i: (jnp.minimum(i, chips - 1), 0)),
            pl.BlockSpec((depth, features), lambda i: (jnp.maximum(i - chips, 0), 0)),
            whole(tokens.shape),
            whole(gain.shape),
        ],
        out_specs=[whole(tokens.shape), whole(tokens.shape)],
        out_shape=[
            jax.ShapeDtypeStruct(tokens.shape, F32),
            jax.ShapeDtypeStruct(tokens.shape, LOW),
        ],
        compiler_params=params(),
        cost_estimate=FREE,
    )(core, mixed, mine, other, tokens, gain)


def row_specs(steps, wholes, pairs, features):
    half = steps // 2

    def spec(first, last, count):
        low = functools.partial(lambda first, last, i: jnp.clip(i - first, 0, last - 1), first, last)
        if count == 2:
            return pl.BlockSpec((ROWS, features), lambda i: (low(i), 0))
        return pl.BlockSpec((None, ROWS, features), lambda i: (0, low(i), 0))

    specs = [spec(0, steps, 2) for _ in wholes]
    for first, second in pairs:
        specs += [spec(0, half, first.ndim), spec(half, half, second.ndim)]
    return specs


def sum_rows(step, steps, count, refs):
    total = sum(ref[...].astype(F32) for ref in refs[:count])
    for i in range(count, len(refs), 2):
        part = jnp.where(step < steps // 2, refs[i][...], refs[i + 1][...])
        total = total + part.astype(F32)
    return total


def norm_back_rows(chips, flipped, d_act, values, gain, upstream):
    d_act = natural_columns(d_act, flipped, chips)
    inverse = lax.rsqrt(jnp.mean(values * values, axis=-1, keepdims=True) + EPS)
    normed = values * inverse
    scaled = d_act * natural_columns(gain, flipped, chips)
    result = upstream + inverse * (
        scaled - normed * jnp.mean(scaled * normed, axis=-1, keepdims=True)
    )
    return result, jnp.sum(d_act * normed, axis=0, keepdims=True)


def middle_kernel(chips, steps, count, size, core, *refs):
    parts, refs = refs[:size], refs[size:]
    resid, gain, d_final, mine, other, d_resid, d_attn, d_mixed, gain_part = refs
    step = pl.program_id(0)
    flipped = core[0] > 0
    tall = resid.shape[0]

    @pl.when(step < steps)
    def _():
        grad, part = norm_back_rows(
            chips,
            flipped,
            sum_rows(step, steps, count, parts),
            resid[...],
            gain[...],
            d_final[...],
        )
        d_resid[...] = grad
        d_attn[pl.ds(pl.multiple_of(step * tall, tall), tall), :] = grad.astype(LOW)

        @pl.when(step == 0)
        def _():
            gain_part[...] = part

        @pl.when(step > 0)
        def _():
            gain_part[...] += part

    @pl.when(step == steps)
    def _():
        gain_part[...] = own_columns(gain_part[...], flipped, chips)

    @pl.when((step >= steps) & (step < steps + chips))
    def _():
        d_mixed[0] = matmul_cols(d_attn[...], mine[...]).astype(LOW)

    @pl.when(step >= steps + chips)
    def _():
        d_mixed[0] = matmul_cols(d_attn[...], other[...]).astype(LOW)


def middle(core, wholes, pairs, resid, gain, d_final, mine, other, chips):
    parts = list(wholes) + [half for pair in pairs for half in pair]
    rows, features = resid.shape
    steps = rows // ROWS
    depth = mine.shape[0] // chips

    def by_rows():
        return pl.BlockSpec((ROWS, features), lambda i: (jnp.minimum(i, steps - 1), 0))

    return pl.pallas_call(
        functools.partial(middle_kernel, chips, steps, len(wholes), len(parts)),
        grid=(steps + 2 * chips,),
        in_specs=[SCALAR]
        + row_specs(steps, wholes, pairs, features)
        + [
            by_rows(),
            whole(gain.shape),
            by_rows(),
            pl.BlockSpec((depth, features), lambda i: (jnp.clip(i - steps, 0, chips - 1), 0)),
            pl.BlockSpec(
                (depth, features), lambda i: (jnp.clip(i - steps - chips, 0, chips - 1), 0)
            ),
        ],
        out_specs=[
            by_rows(),
            whole(resid.shape),
            pl.BlockSpec(
                (1, rows, depth),
                lambda i: (
                    lax.rem(jnp.maximum(i - steps, 0), chips),
                    0,
                    lax.div(jnp.maximum(i - steps, 0), chips),
                ),
            ),
            whole((1, features)),
        ],
        out_shape=[
            jax.ShapeDtypeStruct(resid.shape, F32),
            jax.ShapeDtypeStruct(resid.shape, LOW),
            jax.ShapeDtypeStruct((chips, rows, 2 * depth), LOW),
            jax.ShapeDtypeStruct((1, features), F32),
        ],
        compiler_params=params(),
        cost_estimate=FREE,
    )(core, *parts, resid, gain, d_final, mine, other)


def last_kernel(chips, steps, count, core, *refs):
    parts, refs = refs[:-4], refs[-4:]
    tokens, gain, d_resid, out = refs
    out[...], _ = norm_back_rows(
        chips,
        core[0] > 0,
        sum_rows(pl.program_id(0), steps, count, parts),
        tokens[...].astype(F32),
        gain[...],
        d_resid[...],
    )


def last(core, wholes, pairs, tokens, gain, d_resid, chips):
    parts = list(wholes) + [half for pair in pairs for half in pair]
    rows, features = tokens.shape
    steps = rows // ROWS
    by_rows = pl.BlockSpec((ROWS, features), lambda i: (i, 0))
    return pl.pallas_call(
        functools.partial(last_kernel, chips, steps, len(wholes)),
        grid=(steps,),
        in_specs=[SCALAR]
        + row_specs(steps, wholes, pairs, features)
        + [by_rows, whole(gain.shape), by_rows],
        out_specs=by_rows,
        out_shape=jax.ShapeDtypeStruct(tokens.shape, F32),
        compiler_params=params(),
        cost_estimate=FREE,
    )(core, *parts, tokens, gain, d_resid)


def inner_first_kernel(act, gate, upward, out):
    out[...] = matmul(act[...], jnp.concatenate([gate[...], upward[...]], axis=1)).astype(LOW)


def inner_second_kernel(act, gate, upward, first, hidden, slope_gate, slope_up):
    width = gate.shape[1]
    both = first[...].astype(F32) + matmul(act[...], jnp.concatenate([gate[...], upward[...]], axis=1))
    gate, upward = both[:, :width], both[:, width:]
    sigma = jax.nn.sigmoid(gate)
    silu = gate * sigma
    hidden[...] = (silu * upward).astype(LOW)
    slope_gate[...] = (upward * sigma * (1.0 + gate * (1.0 - sigma))).astype(LOW)
    slope_up[...] = silu.astype(LOW)


def inner_specs(act, weights, part):
    rows = act.shape[0]
    half, columns = weights.shape
    tiles = columns // (2 * LANES)
    return tiles, [
        pl.BlockSpec((rows, half), lambda i: (0, part)),
        pl.BlockSpec((half, LANES), lambda i: (0, i)),
        pl.BlockSpec((half, LANES), lambda i: (0, tiles + i)),
    ]


def inner_first(act, weights):
    rows, columns = act.shape[0], weights.shape[1]
    if columns % (2 * LANES):
        return matmul(act[:, : weights.shape[0]], weights).astype(LOW)
    tiles, specs = inner_specs(act, weights, 0)
    return pl.pallas_call(
        inner_first_kernel,
        grid=(tiles,),
        in_specs=specs,
        out_specs=pl.BlockSpec((rows, 2 * LANES), lambda i: (0, i)),
        out_shape=jax.ShapeDtypeStruct((rows, columns), LOW),
        compiler_params=params(),
        cost_estimate=FREE,
    )(act, weights, weights)


def inner_second(act, weights, first):
    rows, columns = act.shape[0], weights.shape[1]
    width = columns // 2
    if columns % (2 * LANES):
        both = first.astype(F32) + matmul(act[:, weights.shape[0] :], weights)
        gate, upward = both[:, :width], both[:, width:]
        sigma = jax.nn.sigmoid(gate)
        silu = gate * sigma
        slope = upward * sigma * (1.0 + gate * (1.0 - sigma))
        return (silu * upward).astype(LOW), slope.astype(LOW), silu.astype(LOW)
    tiles, specs = inner_specs(act, weights, 1)
    tile = pl.BlockSpec((rows, LANES), lambda i: (0, i))
    return pl.pallas_call(
        inner_second_kernel,
        grid=(tiles,),
        in_specs=specs + [pl.BlockSpec((rows, 2 * LANES), lambda i: (0, i))],
        out_specs=[tile] * 3,
        out_shape=[jax.ShapeDtypeStruct((rows, width), LOW)] * 3,
        compiler_params=params(),
        cost_estimate=FREE,
    )(act, weights, weights, first)


def place_halves(flag, mine, other, out):
    rows = mine.shape[0]
    core = flag[0]
    out[pl.ds(pl.multiple_of(core * rows, 16), rows), :] = mine[...]
    out[pl.ds(pl.multiple_of((1 - core) * rows, 16), rows), :] = other[...]


def inner_back_kernel(flag, d_ffn, mine, other, slope_gate, slope_up, out, down):
    @pl.when(pl.program_id(0) == 0)
    def _():
        place_halves(flag, mine, other, down)

    width = down.shape[0]
    d_hidden = matmul_cols(d_ffn[...], down[...])
    out[:, :width] = (d_hidden * slope_gate[...]).astype(LOW)
    out[:, width:] = (d_hidden * slope_up[...]).astype(LOW)


def inner_back(flag, d_ffn, mine, other, slope_gate, slope_up, chips):
    rows, features = d_ffn.shape
    width = 2 * mine.shape[0]
    if width % LANES:
        d_hidden = matmul_cols(d_ffn, core_rows(mine, other))
        return jnp.concatenate([d_hidden * slope_gate, d_hidden * slope_up], axis=1).astype(LOW)
    tall = rows // chips
    flat = pl.BlockSpec((tall, width), lambda i: (i, 0))
    return pl.pallas_call(
        inner_back_kernel,
        grid=(chips,),
        in_specs=[
            SCALAR,
            pl.BlockSpec((tall, features), lambda i: (i, 0)),
            whole(mine.shape),
            whole(other.shape),
            flat,
            flat,
        ],
        out_specs=pl.BlockSpec((tall, 2 * width), lambda i: (i, 0)),
        out_shape=jax.ShapeDtypeStruct((rows, 2 * width), LOW),
        scratch_shapes=[pltpu.VMEM((width, features), LOW)],
        compiler_params=params(60),
        cost_estimate=FREE,
    )(flag, d_ffn, mine, other, slope_gate, slope_up)


def back_project_kernel(tiles, chips, d_out, mine, other, *refs):
    act, outs, total = (refs[0], refs[1:-1], refs[-1]) if chips == 0 else (None, refs, None)
    step = pl.program_id(0)
    columns = d_out.shape[1]

    def work(weights):
        grad = matmul_cols(d_out[...], weights[:, :columns])
        if act is not None:
            total[...] = jnp.sum(grad * act[...].astype(F32), axis=0, keepdims=True)
        spread(grad.astype(LOW), outs)

    @pl.when(step < tiles)
    def _():
        work(mine)

    @pl.when(step >= tiles)
    def _():
        work(other)


def back_project(d_out, mine, other, chips, *act):
    rows, columns = d_out.shape
    half = mine.shape[0]
    tile = 2 * LANES
    tiles = half // tile
    shapes = spread_shapes(chips, rows, 2 * half)
    flat = pl.BlockSpec((rows, tile), lambda i: (0, i))
    outs = pl.pallas_call(
        functools.partial(back_project_kernel, tiles, 0 if act else 1),
        grid=(2 * tiles,),
        in_specs=[
            whole(d_out.shape),
            pl.BlockSpec((tile, mine.shape[1]), lambda i: (jnp.minimum(i, tiles - 1), 0)),
            pl.BlockSpec((tile, mine.shape[1]), lambda i: (jnp.maximum(i - tiles, 0), 0)),
        ]
        + [flat for _ in act],
        out_specs=[column_spec(shape, tile) for shape in shapes]
        + [pl.BlockSpec((1, tile), lambda i: (0, i)) for _ in act],
        out_shape=[jax.ShapeDtypeStruct(shape, LOW) for shape in shapes]
        + [jax.ShapeDtypeStruct((1, 2 * half), F32) for _ in act],
        compiler_params=params(40),
        cost_estimate=FREE,
    )(d_out, mine, other, *act)
    return (outs[:-1], outs[-1]) if act else outs


def turned_kernel(count, left, right, *refs):
    arrived, outs = refs[:count], refs[count:]
    total = matmul_rows(left[...], right[...])
    if arrived:
        total = total + arrived[0][...].astype(F32)
    spread(total.astype(LOW), outs)


def turned(left, part, right, *arrived, chips=1):
    rows, half = left.shape[0], left.shape[1] // CORES
    width = right.shape[1]
    tile = LANES if width % (2 * LANES) else 2 * LANES
    shapes = spread_shapes(chips, half, width)
    outs = pl.pallas_call(
        functools.partial(turned_kernel, len(arrived)),
        grid=(width // tile,),
        in_specs=[
            pl.BlockSpec((rows, half), lambda i: (0, part)),
            pl.BlockSpec((rows, tile), lambda i: (0, i)),
        ]
        + [pl.BlockSpec((half, tile), lambda i: (0, i)) for _ in arrived],
        out_specs=[column_spec(shape, tile) for shape in shapes],
        out_shape=[jax.ShapeDtypeStruct(shape, LOW) for shape in shapes],
        compiler_params=params(60 if width > half * 2 else 32),
        cost_estimate=FREE,
    )(left, right, *arrived)
    return outs[0] if chips == 1 else outs


def inner_out_kernel(flag, left, mine, other, *refs):
    outs, down = refs[:-1], refs[-1]
    step = pl.program_id(0)

    @pl.when(step == 0)
    def _():
        place_halves(flag, mine, other, down)

    spread_step(step, matmul(left[...], down[...]).astype(LOW), outs)


def inner_out(flag, hidden, mine, other, chips):
    rows, width = hidden.shape
    features = mine.shape[1]
    if width % LANES:
        return [matmul(hidden, core_rows(mine, other)).astype(LOW)]
    tall = rows // chips
    shapes = spread_shapes(chips, rows, features)
    flat = pl.BlockSpec((tall, features), lambda i: (i, 0))
    return pl.pallas_call(
        inner_out_kernel,
        grid=(chips,),
        in_specs=[
            SCALAR,
            pl.BlockSpec((tall, width), lambda i: (i, 0)),
            whole(mine.shape),
            whole(other.shape),
        ],
        out_specs=[flat] if len(shapes) == 1 else [whole(shape) for shape in shapes],
        out_shape=[jax.ShapeDtypeStruct(shape, LOW) for shape in shapes],
        scratch_shapes=[pltpu.VMEM((width, features), LOW)],
        compiler_params=params(36),
        cost_estimate=FREE,
    )(flag, hidden, mine, other)


def half_kernel(flag, left, right, *refs):
    arrived, out = refs[:-1], refs[-1]
    rows = out.shape[0]
    start = left.shape[1] - rows
    wide = -(-rows // LANES) * LANES
    second = flag[0] > 0
    first = pl.multiple_of(jnp.where(second, left.shape[1] - wide, 0), LANES)
    total = matmul_rows(left[:, pl.ds(first, wide)], right[...])
    total = jnp.where(second, total[wide - rows :], total[:rows])
    if arrived:
        total = total + arrived[0][...].astype(F32)
    out[...] = total.astype(LOW)


def half_product(flag, left, right, *arrived):
    rows, columns = left.shape
    width = right.shape[1]
    half = columns // 2
    if columns % LANES:
        total = matmul_rows(left, right)
        total = jnp.where(flag[0] > 0, total[half:], total[:half])
        return sum([part.astype(F32) for part in arrived], total).astype(LOW)
    tile = 2 * LANES
    return pl.pallas_call(
        half_kernel,
        grid=(width // tile,),
        in_specs=[SCALAR, whole(left.shape), pl.BlockSpec((rows, tile), lambda i: (0, i))]
        + [pl.BlockSpec((half, tile), lambda i: (0, i)) for _ in arrived],
        out_specs=pl.BlockSpec((half, tile), lambda i: (0, i)),
        out_shape=jax.ShapeDtypeStruct((half, width), LOW),
        compiler_params=params(60),
        cost_estimate=FREE,
    )(flag, left, right, *arrived)


def per_device(
    tokens,
    out_cotangent,
    group_ids,
    attn_gain,
    query_weight,
    key_weight,
    value_weight,
    out_weight,
    ffn_gain,
    gate_weight,
    up_weight,
    down_weight,
):
    tok_count, features = tokens.shape[1:]
    weight_rows, inner = gate_weight.shape
    chips = chip_count()
    chip, core = own_chip(), own_core()
    ids = lax.iota(jnp.int32, chips)
    head_width, inner_width = features // chips, inner // chips
    half = features // CORES
    flag = jnp.full((1,), core, jnp.int32)
    tokens, out_cotangent = tokens[0], out_cotangent[0]

    gains = jnp.concatenate(
        [
            jnp.broadcast_to(attn_gain[:, None], (weight_rows, LANES // 2)),
            jnp.broadcast_to(ffn_gain[:, None], (weight_rows, LANES // 2)),
        ],
        axis=1,
    )

    def for_chip(weight, k):
        width = weight.shape[1] // chips
        return lax.dynamic_slice_in_dim(weight, (chip ^ k) * width, width, axis=1)

    def rows_of_chips(weights, *others):
        parts = [jnp.concatenate([for_chip(w, k) for w in weights], axis=1) for k in range(chips)]
        parts = [jnp.concatenate([part] + list(others), axis=1) for part in parts]
        return jnp.stack(in_order(chips_scatter(parts)))

    group_span = GPS * lax.axis_size("batch")
    onehot = (group_ids[0, :, None] == jnp.arange(group_span, dtype=jnp.int32)[None, :]).astype(F32)
    group_total = seq_sum(jnp.sum(onehot, axis=0, keepdims=True))
    own_total = jnp.sum(onehot * group_total, axis=-1)[:, None]
    weighting = tok_count * lax.axis_size("seq") / (GPS * own_total)
    d_final = out_cotangent.astype(F32) * weighting

    out_mine = batch_gather(out_weight, 0)
    qkv_rows = rows_of_chips([query_weight, key_weight, value_weight], gains)
    qkv_mine = batch_gather(after(qkv_rows, out_mine), 1).reshape(half, -1)
    tokens_sent = after(tokens, qkv_rows, group_total)
    tokens_near = gather_near(tokens_sent)
    tokens_far = gather_far(tokens_near)
    gathered = gathered_rows(tokens_sent, tokens_near, tokens_far)
    ffn_sent = after(d_final.astype(LOW), *tokens_near, *tokens_far)
    ffn_near = gather_near(ffn_sent)
    gate_weight, up_weight = after((gate_weight, up_weight), gathered)
    inner_rows = rows_of_chips([gate_weight, up_weight])
    inner_mine = batch_gather(inner_rows, 1).reshape(half, -1)
    down_mine = batch_gather(after(down_weight, inner_rows), 0)

    ffn_far = gather_far(ffn_near)
    out_sent = after(out_mine, inner_rows)
    out_near = gather_near(out_sent)
    qkv_mine = after(qkv_mine, inner_rows, *ffn_near)
    qkv_other = swap_core(qkv_mine)
    out_far = gather_far(out_near)
    columns = 3 * head_width
    gain_one, gain_two = (
        jnp.concatenate([qkv_mine[:, place], qkv_other[:, place]]).astype(F32)[None]
        for place in (columns, columns + LANES // 2)
    )
    act_one, qkv = project(flag, gathered, gain_one, qkv_mine, qkv_other, columns, chips)
    qkv = qkv.reshape(chips, tok_count, columns)
    place = chip ^ ids
    tails = swap_core(qkv[:, tok_count - WINDOW :, head_width:])
    before = jnp.where(core > 0, ids, chip ^ jnp.maximum(place - 1, 0))
    follow = jnp.where(core > 0, chip ^ jnp.minimum(place + 1, chips - 1), ids)
    preceded = ((core > 0) | (place > 0)).astype(jnp.int32)
    followed = (core == 0) | (place < chips - 1)
    rims = jnp.take(after(tails, *out_near), before, axis=0)
    mixed = attention(flag, preceded, qkv, rims)

    mixed = after(mixed, *out_far, *ffn_far)
    mixed_own = chips_scatter([mixed[k] for k in range(chips)])
    cell = head_width // CORES
    mixed_own = jnp.concatenate(
        [block[:, i * cell : (i + 1) * cell] for i in range(CORES) for block in mixed_own], axis=1
    )
    out_near = after(out_near, mixed)
    out_half = gathered_rows(out_sent, out_near, out_far)
    out_other = swap_core(out_half)
    resid, act_two_own = out_project(
        flag, mixed_own, out_half, out_other, tokens, gain_two, chips
    )

    d_ffn = gathered_rows(ffn_sent, ffn_near, ffn_far)
    act_two_own = after(act_two_own, d_ffn)
    act_near = gather_near(act_two_own)
    act_far = gather_far(after(act_near, inner_mine))
    act_two = gathered_rows(act_two_own, act_near, act_far)
    inner_mine = after(inner_mine, *act_near)
    inner_other = swap_core(inner_mine)
    first = inner_first(act_two, inner_mine)
    hidden, slope_gate, slope_up = inner_second(act_two, inner_other, first)
    down_send = half_product(1 - flag, hidden, d_ffn)
    down_back = swap_core(down_send)
    down_mine = after(down_mine, down_send)
    down_sum = half_product(flag, hidden, after(d_ffn, down_send, down_mine), down_back)
    down_other = swap_core(down_mine)
    down_grad = batch_scatter(down_sum, 0)
    d_gate_up = inner_back(
        flag, after(d_ffn, down_sum), down_mine, down_other, slope_gate, slope_up, chips
    )
    inner_send = matmul_rows(act_two[:, half:], d_gate_up).astype(LOW)
    act_parts = back_project(after(d_gate_up, inner_send), inner_mine, inner_other, chips)
    act_near = chips_sum_near(act_parts)
    inner_sum = turned(
        act_two, 0, after(d_gate_up, act_parts[0], down_grad), swap_core(inner_send)
    )
    act_far = chips_sum_far(act_parts, act_near)
    inner_sum = after(inner_sum, *act_near)
    inner_grad = batch_scatter(inner_sum.reshape(chips, half // chips, -1), 1)
    d_resid, d_attn, d_mixed_own, gain_two_part = middle(
        flag,
        *summands(act_parts, act_near, act_far),
        resid,
        gain_two,
        d_final,
        out_half,
        out_other,
        chips,
    )

    d_mixed_parts = chips_scatter([d_mixed_own[k] for k in range(chips)])
    d_mixed = jnp.stack(d_mixed_parts)
    d_qkv, lent = attention_back(flag, preceded, qkv, rims, d_mixed)
    lent = swap_core(lent)
    block_parts = inner_out(flag, after(hidden, d_mixed_own), down_mine, down_other, chips)
    block_near = chips_sum_near(block_parts)

    returned = jnp.where(followed[:, None, None], jnp.take(lent, follow, axis=0), 0)
    d_qkv = d_qkv.at[:, tok_count - WINDOW :, head_width:].add(returned)
    d_qkv = after(d_qkv.reshape(chips * tok_count, columns), *block_near)
    qkv_send = turned(act_one, 1, d_qkv)
    out_send = turned(mixed_own, 1, after(d_attn, qkv_send))
    out_back = swap_core(out_send)
    between = chips_sum_between(block_parts, after(block_near, qkv_send))
    block_far = chips_sum_send(between)
    qkv_sum = turned(act_one, 0, after(d_qkv, qkv_send, *between), swap_core(qkv_send))
    d_act_parts, gain_one_part = back_project(
        after(d_qkv, qkv_sum), qkv_mine, qkv_other, chips, act_one
    )
    qkv_sum = after(qkv_sum, inner_grad, d_act_parts[0])
    qkv_grad = batch_scatter(qkv_sum.reshape(chips, half // chips, -1), 1)

    out_parts = turned(mixed_own, 0, after(d_attn, d_act_parts[0]), out_back, chips=chips)
    out_parts = out_parts if chips > 1 else [out_parts]
    out_near = chips_sum_near(out_parts)
    gain_parts = jnp.concatenate([gain_one_part / gain_one, gain_two_part], axis=0)
    gain_core = swap_core(gain_parts[:, half:])
    def columns_of_chips(grad):
        chip_rows = [
            lax.dynamic_index_in_dim(grad, chip ^ k, axis=0, keepdims=False) for k in range(chips)
        ]
        return chips_scatter(chip_rows)

    out_far = chips_sum_far(out_parts, out_near)
    inner_cells = columns_of_chips(after(inner_grad, *out_near))
    out_sum = summed(out_parts, out_near, out_far).astype(LOW)
    out_grad = batch_scatter(after(out_sum, qkv_grad), 0)
    d_act_parts = after(d_act_parts, qkv_grad, *out_far, *inner_cells[1:])
    d_act_near = chips_sum_near(d_act_parts)
    gain_grads = (gain_parts[:, :half] + after(gain_core, qkv_grad)).reshape(2, chips, -1)
    gain_grads = chips_scatter(
        [
            lax.dynamic_index_in_dim(gain_grads, chip ^ k, axis=1, keepdims=False)
            for k in range(chips)
        ]
    )
    d_act_far = chips_sum_far(d_act_parts, d_act_near)
    row = lax.axis_index("batch")
    gain_grads = sum(after(gain_grads, *d_act_near))
    gain_grads = gain_grads.reshape(2, lax.axis_size("batch"), -1)
    gain_grads = sum(
        exchange(
            lax.dynamic_index_in_dim(gain_grads, row ^ k, axis=1, keepdims=False), k, "batch"
        )
        for k in range(lax.axis_size("batch"))
    )
    qkv_cells = columns_of_chips(after(qkv_grad, *d_act_near))
    tokens_grad = last(
        flag, *summands(d_act_parts, d_act_near, d_act_far), tokens, gain_one, d_resid, chips
    )
    block_out = (resid + summed(block_parts, block_near, block_far)).astype(LOW)

    inner_grad, qkv_grad = in_order(inner_cells), in_order(qkv_cells)

    def whole_columns(blocks, first, width):
        parts = [block[:, first : first + width] for block in blocks]
        return jnp.concatenate(parts, axis=1).astype(F32)


    return (
        block_out[None],
        tokens_grad[None],
        gain_grads[0],
        whole_columns(qkv_grad, 0, head_width),
        whole_columns(qkv_grad, head_width, head_width),
        whole_columns(qkv_grad, 2 * head_width, head_width),
        out_grad.astype(F32),
        gain_grads[1],
        whole_columns(inner_grad, 0, inner_width),
        whole_columns(inner_grad, inner_width, inner_width),
        down_grad.astype(F32),
    )


def solution(mesh):
    rows = P(("seq", "batch"), None)
    vector = P(("seq", "batch"))
    cells = P("batch", "seq", None)
    return jax.shard_map(
        per_device,
        mesh=mesh,
        in_specs=(cells, cells, P("batch", "seq"))
        + (vector, rows, rows, rows, rows, vector, rows, rows, rows),
        out_specs=(cells, cells, vector, rows, rows, rows, rows, vector, rows, rows, rows),
        check_vma=False,
    )
```

```python
import functools

import jax
import jax.numpy as jnp
from jax import lax
from jax.experimental import pallas as pl
from jax.experimental.pallas import tpu as pltpu
from jax.sharding import PartitionSpec as P

HEAD = 128
WINDOW = 64
GPS = 4
CORES = 2

EPS = 1e-05
NEGATIVE = -1e30
ROWS_DIMS = (((0,), (0,)), ((), ()))
COLS_DIMS = (((1,), (1,)), ((), ()))
BLOCK = 128
ROWS = 64
LANES = 128
F32 = jnp.float32
LOW = jnp.bfloat16


def matmul(left, right):
    return jnp.dot(left, right, preferred_element_type=F32)


def matmul_rows(left, right):
    return lax.dot_general(left, right, ROWS_DIMS, preferred_element_type=F32)


def matmul_cols(left, right):
    return lax.dot_general(left, right, COLS_DIMS, preferred_element_type=F32)


def exchange(value, flip, axis="seq"):
    if flip == 0:
        return value
    count = lax.axis_size(axis)
    return lax.ppermute(value, axis, [(place, place ^ flip) for place in range(count)])


def swap_core(value):
    return exchange(value, 1)


def chip_count():
    return lax.axis_size("seq") // CORES


def own_chip():
    return lax.axis_index("seq") // CORES


def own_core():
    return lax.axis_index("seq") % CORES


def gather_near(value):
    if chip_count() != 4:
        return [exchange(value, CORES * k) for k in range(1, chip_count())]
    return [exchange(value, CORES), exchange(value, 2 * CORES)]


def gather_far(near):
    if chip_count() != 4:
        return []
    half = near[0].shape[0] // 2
    return [exchange(near[0][:half], 2 * CORES), exchange(near[1][half:], CORES)]


def gathered_rows(value, near, far):
    return jnp.concatenate([value] + near + far, axis=0)


def chips_scatter(blocks):
    return [blocks[0]] + [exchange(blocks[k], CORES * k) for k in range(1, chip_count())]


def chips_sum_near(parts):
    if chip_count() != 4:
        blocks = parts[0].reshape((chip_count(), -1) + parts[0].shape[1:])
        return chips_scatter([blocks[k] for k in range(chip_count())])
    return [exchange(parts[1], CORES), exchange(parts[2], 2 * CORES)]


def chips_sum_between(parts, near):
    if chip_count() != 4:
        return []
    on_second = (parts[3].astype(F32) + near[0][1].astype(F32)).astype(LOW)
    on_first = (parts[4].astype(F32) + near[1][1].astype(F32)).astype(LOW)
    return [on_second, on_first]


def chips_sum_far(parts, near):
    return chips_sum_send(chips_sum_between(parts, near))


def chips_sum_send(between):
    return [exchange(part, step * CORES) for part, step in zip(between, (2, 1))]


def summands(parts, near, far):
    if not far:
        return near, []
    return [parts[0]], [(near[0][0], near[1][0]), tuple(far)]


def summed(parts, near, far):
    wholes, pairs = summands(parts, near, far)
    total = sum(part.astype(F32) for part in wholes)
    return total + sum(jnp.concatenate(pair, axis=0).astype(F32) for pair in pairs)


def spread_shapes(chips, rows, columns):
    if chips != 4:
        return [(rows, columns)]
    tall, low = rows // chips, rows // chips // 2
    return [(tall, columns), (2, low, columns), (2, low, columns), (low, columns), (low, columns)]


def spread_block(block, value, outs, place=slice(None)):
    own, first, second, keep_second, keep_first = outs
    low = value.shape[0] // 2
    if block == 0:
        own[:, place] = value
    if block == 1:
        first[0, :, place] = value[:low]
        keep_first[:, place] = value[low:]
    if block == 2:
        keep_second[:, place] = value[:low]
        second[0, :, place] = value[low:]
    if block == 3:
        first[1, :, place] = value[:low]
        second[1, :, place] = value[low:]


def spread(total, outs):
    if len(outs) == 1:
        outs[0][...] = total
        return
    tall = total.shape[0] // 4
    for block in range(4):
        spread_block(block, total[block * tall : (block + 1) * tall], outs)


def column_spec(shape, tile):
    lead = (0,) * (len(shape) - 1)
    return pl.BlockSpec(shape[:-1] + (tile,), lambda i: lead + (i,))


def spread_step(step, value, outs, place=slice(None)):
    if len(outs) == 1:
        outs[0][:, place] = value
        return
    for block in range(4):

        @pl.when(step == block)
        def _():
            spread_block(block, value, outs, place)


def in_order(blocks):
    chip = own_chip()
    bit = 1
    while bit < len(blocks):
        flipped = (chip & bit) > 0
        blocks = [jnp.where(flipped, blocks[i ^ bit], blocks[i]) for i in range(len(blocks))]
        bit *= 2
    return blocks


def to_chips(value):
    chip = own_chip()
    blocks = [
        lax.dynamic_index_in_dim(value, chip ^ k, axis=0, keepdims=False)
        for k in range(chip_count())
    ]
    return jnp.stack(in_order(chips_scatter(blocks)))


def after(value, *others):
    return lax.optimization_barrier((value,) + others)[0]


def seq_sum(value):
    bit = 1
    while bit < lax.axis_size("seq"):
        value = value + exchange(value, bit)
        bit *= 2
    return value


def own_first(first, second):
    flipped = own_core() > 0
    return jnp.where(flipped, second, first), jnp.where(flipped, first, second)


def core_rows(mine, other):
    return jnp.concatenate(own_first(mine, other), axis=0)


def batch_gather(value, axis):
    return lax.all_gather(value, "batch", axis=axis, tiled=True)


def batch_scatter(value, axis):
    return lax.psum_scatter(value, "batch", scatter_dimension=axis, tiled=True)


FREE = pl.CostEstimate(flops=0, bytes_accessed=0, transcendentals=0)


def params(megabytes=32):
    return pltpu.CompilerParams(vmem_limit_bytes=megabytes * 2**20)


def whole(shape):
    return pl.BlockSpec(shape, lambda *step: (0,) * len(shape))


SCALAR = pl.BlockSpec(memory_space=pltpu.SMEM)


def own_columns(values, flipped, chips):
    width = values.shape[1] // (chips * CORES)
    cells = [values[:, i * width : (i + 1) * width] for i in range(chips * CORES)]
    mine = [jnp.where(flipped, cells[2 * q + 1], cells[2 * q]) for q in range(chips)]
    other = [jnp.where(flipped, cells[2 * q], cells[2 * q + 1]) for q in range(chips)]
    return jnp.concatenate(mine + other, axis=1)


def natural_columns(values, flipped, chips):
    width = values.shape[1] // (chips * CORES)
    cells = [values[:, i * width : (i + 1) * width] for i in range(chips * CORES)]
    pairs = []
    for q in range(chips):
        mine, other = cells[q], cells[chips + q]
        pairs += [jnp.where(flipped, other, mine), jnp.where(flipped, mine, other)]
    return jnp.concatenate(pairs, axis=1)


def project_kernel(chips, core, tokens, gain, mine, other, act, out):
    flipped = core[0] > 0
    half, columns = mine.shape[0], out.shape[1]

    @pl.loop(0, tokens.shape[0], step=ROWS)
    def _(start):
        rows = pl.ds(pl.multiple_of(start, ROWS), ROWS)
        values = tokens[rows, :].astype(F32)
        inverse = lax.rsqrt(jnp.mean(values * values, axis=-1, keepdims=True) + EPS)
        act[rows, :] = (own_columns(values * inverse, flipped, chips) * gain[...]).astype(LOW)

    total = matmul(act[:, :half], mine[:, :columns]) + matmul(act[:, half:], other[:, :columns])
    out[...] = total.astype(LOW)


def project(core, tokens, gain, mine, other, columns, chips):
    rows, features = tokens.shape
    tall = rows // chips
    return pl.pallas_call(
        functools.partial(project_kernel, chips),
        grid=(chips,),
        in_specs=[
            SCALAR,
            pl.BlockSpec((tall, features), lambda i: (i, 0)),
            whole(gain.shape),
            whole(mine.shape),
            whole(other.shape),
        ],
        out_specs=[
            pl.BlockSpec((tall, features), lambda i: (i, 0)),
            pl.BlockSpec((tall, columns), lambda i: (i, 0)),
        ],
        out_shape=[
            jax.ShapeDtypeStruct((rows, features), LOW),
            jax.ShapeDtypeStruct((rows, columns), LOW),
        ],
        compiler_params=params(40),
        cost_estimate=FREE,
    )(core, tokens, gain, mine, other)


def windows(keys, rim, step):
    if step == 0:
        return jnp.concatenate([rim, keys[:BLOCK]], axis=0)
    return keys[step * BLOCK - WINDOW : (step + 1) * BLOCK]


def window_probs(queries, keys, first, preceded):
    scores = matmul_cols(queries, keys) * HEAD ** (-0.5)
    query = lax.broadcasted_iota(jnp.int32, scores.shape, 0)
    key = lax.broadcasted_iota(jnp.int32, scores.shape, 1)
    allowed = (key > query) & (key <= query + WINDOW)
    if first:
        allowed = allowed & ((key >= WINDOW) | (preceded > 0))
    scores = jnp.where(allowed, scores, NEGATIVE)
    expo = jnp.exp(scores - jnp.max(scores, axis=-1, keepdims=True))
    return expo / jnp.sum(expo, axis=-1, keepdims=True)


def attend_kernel(core, preceded, qkv, rim, out):
    flipped = core[0] > 0
    ready = preceded[pl.program_id(0)]
    width = out.shape[2]
    heads = width // HEAD
    mixed = []
    for head in range(heads):
        cell = slice(head * HEAD, (head + 1) * HEAD)
        queries, keys, values = (
            qkv[0, :, part * width + head * HEAD : part * width + (head + 1) * HEAD]
            for part in range(3)
        )
        rim_keys = rim[0, :, cell]
        rim_values = rim[0, :, width + head * HEAD : width + (head + 1) * HEAD]
        rows = []
        for step in range(queries.shape[0] // BLOCK):
            probs = window_probs(
                queries[step * BLOCK : (step + 1) * BLOCK],
                windows(keys, rim_keys, step),
                step == 0,
                ready,
            )
            rows.append(matmul(probs.astype(LOW), windows(values, rim_values, step)))
        mixed.append(jnp.concatenate(rows, axis=0).astype(LOW))
    half = heads // CORES
    for head in range(half):
        first, second = mixed[head], mixed[half + head]
        out[0, :, head * HEAD : (head + 1) * HEAD] = jnp.where(flipped, second, first)
        out[0, :, (half + head) * HEAD : (half + head + 1) * HEAD] = jnp.where(
            flipped, first, second
        )


def attention(core, preceded, qkv, rims):
    chips, rows, columns = qkv.shape
    width = columns // 3
    return pl.pallas_call(
        attend_kernel,
        grid=(chips,),
        in_specs=[
            SCALAR,
            SCALAR,
            pl.BlockSpec((1, rows, columns), lambda i: (i, 0, 0)),
            pl.BlockSpec((1,) + rims.shape[1:], lambda i: (i, 0, 0)),
        ],
        out_specs=pl.BlockSpec((1, rows, width), lambda i: (i, 0, 0)),
        out_shape=jax.ShapeDtypeStruct((chips, rows, width), LOW),
        compiler_params=params(),
        cost_estimate=FREE,
    )(core, preceded, qkv, rims)


def attend_back_kernel(core, preceded, qkv, rim, d_mixed, out, lent):
    flipped = core[0] > 0
    ready = preceded[pl.program_id(0)]
    width = d_mixed.shape[2]
    heads = width // HEAD
    half = heads // CORES
    factor = HEAD ** (-0.5)
    for head in range(heads):
        queries, keys, values = (
            qkv[0, :, part * width + head * HEAD : part * width + (head + 1) * HEAD]
            for part in range(3)
        )
        rim_keys = rim[0, :, head * HEAD : (head + 1) * HEAD]
        rim_values = rim[0, :, width + head * HEAD : width + (head + 1) * HEAD]
        there = (head + half) % heads
        upstream = jnp.where(
            flipped,
            d_mixed[0, :, there * HEAD : (there + 1) * HEAD],
            d_mixed[0, :, head * HEAD : (head + 1) * HEAD],
        )
        steps = queries.shape[0] // BLOCK
        d_queries, d_keys, d_values = [], [], []
        for step in range(steps):
            rows = slice(step * BLOCK, (step + 1) * BLOCK)
            near_keys, near_values = windows(keys, rim_keys, step), windows(values, rim_values, step)
            probs = window_probs(queries[rows], near_keys, step == 0, ready)
            d_probs = matmul_cols(upstream[rows], near_values)
            d_scores = probs * (d_probs - jnp.sum(probs * d_probs, axis=-1, keepdims=True))
            d_scores = d_scores.astype(LOW)
            d_queries.append(matmul(d_scores, near_keys) * factor)
            d_keys.append(matmul_rows(d_scores, queries[rows]) * factor)
            d_values.append(matmul_rows(probs.astype(LOW), upstream[rows]))
        out[0, :, head * HEAD : (head + 1) * HEAD] = jnp.concatenate(d_queries, axis=0).astype(LOW)
        for part, grads in ((1, d_keys), (2, d_values)):
            first = (part - 1) * width + head * HEAD
            lent[0, :, first : first + HEAD] = grads[0][:WINDOW].astype(LOW)
            for step in range(steps):
                own = grads[step][WINDOW:]
                if step + 1 < steps:
                    keep = own[: BLOCK - WINDOW]
                    own = jnp.concatenate(
                        [keep, own[BLOCK - WINDOW :] + grads[step + 1][:WINDOW]], axis=0
                    )
                out[
                    0,
                    step * BLOCK : (step + 1) * BLOCK,
                    part * width + head * HEAD : part * width + (head + 1) * HEAD,
                ] = own.astype(LOW)


def attention_back(core, preceded, qkv, rims, d_mixed):
    chips, rows, columns = qkv.shape
    width = columns // 3
    return pl.pallas_call(
        attend_back_kernel,
        grid=(chips,),
        in_specs=[
            SCALAR,
            SCALAR,
            pl.BlockSpec((1, rows, columns), lambda i: (i, 0, 0)),
            pl.BlockSpec((1,) + rims.shape[1:], lambda i: (i, 0, 0)),
            pl.BlockSpec((1, rows, width), lambda i: (i, 0, 0)),
        ],
        out_specs=[
            pl.BlockSpec((1, rows, columns), lambda i: (i, 0, 0)),
            pl.BlockSpec((1,) + rims.shape[1:], lambda i: (i, 0, 0)),
        ],
        out_shape=[
            jax.ShapeDtypeStruct(qkv.shape, LOW),
            jax.ShapeDtypeStruct(rims.shape, LOW),
        ],
        compiler_params=params(),
        cost_estimate=FREE,
    )(core, preceded, qkv, rims, d_mixed)


def out_kernel(chips, core, mixed, mine, other, tokens, gain, resid, act):
    step, steps = pl.program_id(0), pl.num_programs(0)
    flipped = core[0] > 0

    @pl.when(step == 0)
    def _():
        resid[...] = tokens[...].astype(F32)

    @pl.when(step < steps // 2)
    def _():
        resid[...] += matmul(mixed[...], mine[...])

    @pl.when(step >= steps // 2)
    def _():
        resid[...] += matmul(mixed[...], other[...])

    @pl.when(step == steps - 1)
    def _():
        @pl.loop(0, tokens.shape[0], step=ROWS)
        def _(start):
            rows = pl.ds(pl.multiple_of(start, ROWS), ROWS)
            values = resid[rows, :]
            inverse = lax.rsqrt(jnp.mean(values * values, axis=-1, keepdims=True) + EPS)
            normed = own_columns(values * inverse, flipped, chips)
            act[rows, :] = (normed * gain[...]).astype(LOW)


def out_project(core, mixed, mine, other, tokens, gain, chips):
    rows, features = tokens.shape
    depth = mine.shape[0] // chips
    return pl.pallas_call(
        functools.partial(out_kernel, chips),
        grid=(2 * chips,),
        in_specs=[
            SCALAR,
            pl.BlockSpec((rows, depth), lambda i: (0, i)),
            pl.BlockSpec((depth, features), lambda i: (jnp.minimum(i, chips - 1), 0)),
            pl.BlockSpec((depth, features), lambda i: (jnp.maximum(i - chips, 0), 0)),
            whole(tokens.shape),
            whole(gain.shape),
        ],
        out_specs=[whole(tokens.shape), whole(tokens.shape)],
        out_shape=[
            jax.ShapeDtypeStruct(tokens.shape, F32),
            jax.ShapeDtypeStruct(tokens.shape, LOW),
        ],
        compiler_params=params(),
        cost_estimate=FREE,
    )(core, mixed, mine, other, tokens, gain)


def row_specs(steps, wholes, pairs, features):
    half = steps // 2

    def spec(first, last, count):
        low = functools.partial(lambda first, last, i: jnp.clip(i - first, 0, last - 1), first, last)
        if count == 2:
            return pl.BlockSpec((ROWS, features), lambda i: (low(i), 0))
        return pl.BlockSpec((None, ROWS, features), lambda i: (0, low(i), 0))

    specs = [spec(0, steps, 2) for _ in wholes]
    for first, second in pairs:
        specs += [spec(0, half, first.ndim), spec(half, half, second.ndim)]
    return specs


def sum_rows(step, steps, count, refs):
    total = sum(ref[...].astype(F32) for ref in refs[:count])
    for i in range(count, len(refs), 2):
        part = jnp.where(step < steps // 2, refs[i][...], refs[i + 1][...])
        total = total + part.astype(F32)
    return total


def norm_back_rows(chips, flipped, d_act, values, gain, upstream):
    d_act = natural_columns(d_act, flipped, chips)
    inverse = lax.rsqrt(jnp.mean(values * values, axis=-1, keepdims=True) + EPS)
    normed = values * inverse
    scaled = d_act * natural_columns(gain, flipped, chips)
    result = upstream + inverse * (
        scaled - normed * jnp.mean(scaled * normed, axis=-1, keepdims=True)
    )
    return result, jnp.sum(d_act * normed, axis=0, keepdims=True)


def middle_kernel(chips, steps, count, size, core, *refs):
    parts, refs = refs[:size], refs[size:]
    resid, gain, d_final, mine, other, d_resid, d_attn, d_mixed, gain_part = refs
    step = pl.program_id(0)
    flipped = core[0] > 0
    tall = resid.shape[0]

    @pl.when(step < steps)
    def _():
        grad, part = norm_back_rows(
            chips,
            flipped,
            sum_rows(step, steps, count, parts),
            resid[...],
            gain[...],
            d_final[...],
        )
        d_resid[...] = grad
        d_attn[pl.ds(pl.multiple_of(step * tall, tall), tall), :] = grad.astype(LOW)

        @pl.when(step == 0)
        def _():
            gain_part[...] = part

        @pl.when(step > 0)
        def _():
            gain_part[...] += part

    @pl.when(step == steps)
    def _():
        gain_part[...] = own_columns(gain_part[...], flipped, chips)

    @pl.when((step >= steps) & (step < steps + chips))
    def _():
        d_mixed[0] = matmul_cols(d_attn[...], mine[...]).astype(LOW)

    @pl.when(step >= steps + chips)
    def _():
        d_mixed[0] = matmul_cols(d_attn[...], other[...]).astype(LOW)


def middle(core, wholes, pairs, resid, gain, d_final, mine, other, chips):
    parts = list(wholes) + [half for pair in pairs for half in pair]
    rows, features = resid.shape
    steps = rows // ROWS
    depth = mine.shape[0] // chips

    def by_rows():
        return pl.BlockSpec((ROWS, features), lambda i: (jnp.minimum(i, steps - 1), 0))

    return pl.pallas_call(
        functools.partial(middle_kernel, chips, steps, len(wholes), len(parts)),
        grid=(steps + 2 * chips,),
        in_specs=[SCALAR]
        + row_specs(steps, wholes, pairs, features)
        + [
            by_rows(),
            whole(gain.shape),
            by_rows(),
            pl.BlockSpec((depth, features), lambda i: (jnp.clip(i - steps, 0, chips - 1), 0)),
            pl.BlockSpec(
                (depth, features), lambda i: (jnp.clip(i - steps - chips, 0, chips - 1), 0)
            ),
        ],
        out_specs=[
            by_rows(),
            whole(resid.shape),
            pl.BlockSpec(
                (1, rows, depth),
                lambda i: (
                    lax.rem(jnp.maximum(i - steps, 0), chips),
                    0,
                    lax.div(jnp.maximum(i - steps, 0), chips),
                ),
            ),
            whole((1, features)),
        ],
        out_shape=[
            jax.ShapeDtypeStruct(resid.shape, F32),
            jax.ShapeDtypeStruct(resid.shape, LOW),
            jax.ShapeDtypeStruct((chips, rows, 2 * depth), LOW),
            jax.ShapeDtypeStruct((1, features), F32),
        ],
        compiler_params=params(),
        cost_estimate=FREE,
    )(core, *parts, resid, gain, d_final, mine, other)


def last_kernel(chips, steps, count, core, *refs):
    parts, refs = refs[:-4], refs[-4:]
    tokens, gain, d_resid, out = refs
    out[...], _ = norm_back_rows(
        chips,
        core[0] > 0,
        sum_rows(pl.program_id(0), steps, count, parts),
        tokens[...].astype(F32),
        gain[...],
        d_resid[...],
    )


def last(core, wholes, pairs, tokens, gain, d_resid, chips):
    parts = list(wholes) + [half for pair in pairs for half in pair]
    rows, features = tokens.shape
    steps = rows // ROWS
    by_rows = pl.BlockSpec((ROWS, features), lambda i: (i, 0))
    return pl.pallas_call(
        functools.partial(last_kernel, chips, steps, len(wholes)),
        grid=(steps,),
        in_specs=[SCALAR]
        + row_specs(steps, wholes, pairs, features)
        + [by_rows, whole(gain.shape), by_rows],
        out_specs=by_rows,
        out_shape=jax.ShapeDtypeStruct(tokens.shape, F32),
        compiler_params=params(),
        cost_estimate=FREE,
    )(core, *parts, tokens, gain, d_resid)


def inner_first_kernel(act, gate, upward, out):
    out[...] = matmul(act[...], jnp.concatenate([gate[...], upward[...]], axis=1)).astype(LOW)


def inner_second_kernel(act, gate, upward, first, hidden, slope_gate, slope_up):
    width = gate.shape[1]
    both = first[...].astype(F32) + matmul(act[...], jnp.concatenate([gate[...], upward[...]], axis=1))
    gate, upward = both[:, :width], both[:, width:]
    sigma = jax.nn.sigmoid(gate)
    silu = gate * sigma
    hidden[...] = (silu * upward).astype(LOW)
    slope_gate[...] = (upward * sigma * (1.0 + gate * (1.0 - sigma))).astype(LOW)
    slope_up[...] = silu.astype(LOW)


def inner_specs(act, weights, part):
    rows = act.shape[0]
    half, columns = weights.shape
    tiles = columns // (2 * LANES)
    return tiles, [
        pl.BlockSpec((rows, half), lambda i: (0, part)),
        pl.BlockSpec((half, LANES), lambda i: (0, i)),
        pl.BlockSpec((half, LANES), lambda i: (0, tiles + i)),
    ]


def inner_first(act, weights):
    rows, columns = act.shape[0], weights.shape[1]
    if columns % (2 * LANES):
        return matmul(act[:, : weights.shape[0]], weights).astype(LOW)
    tiles, specs = inner_specs(act, weights, 0)
    return pl.pallas_call(
        inner_first_kernel,
        grid=(tiles,),
        in_specs=specs,
        out_specs=pl.BlockSpec((rows, 2 * LANES), lambda i: (0, i)),
        out_shape=jax.ShapeDtypeStruct((rows, columns), LOW),
        compiler_params=params(),
        cost_estimate=FREE,
    )(act, weights, weights)


def inner_second(act, weights, first):
    rows, columns = act.shape[0], weights.shape[1]
    width = columns // 2
    if columns % (2 * LANES):
        both = first.astype(F32) + matmul(act[:, weights.shape[0] :], weights)
        gate, upward = both[:, :width], both[:, width:]
        sigma = jax.nn.sigmoid(gate)
        silu = gate * sigma
        slope = upward * sigma * (1.0 + gate * (1.0 - sigma))
        return (silu * upward).astype(LOW), slope.astype(LOW), silu.astype(LOW)
    tiles, specs = inner_specs(act, weights, 1)
    tile = pl.BlockSpec((rows, LANES), lambda i: (0, i))
    return pl.pallas_call(
        inner_second_kernel,
        grid=(tiles,),
        in_specs=specs + [pl.BlockSpec((rows, 2 * LANES), lambda i: (0, i))],
        out_specs=[tile] * 3,
        out_shape=[jax.ShapeDtypeStruct((rows, width), LOW)] * 3,
        compiler_params=params(),
        cost_estimate=FREE,
    )(act, weights, weights, first)


def place_halves(flag, mine, other, out):
    rows = mine.shape[0]
    core = flag[0]
    out[pl.ds(pl.multiple_of(core * rows, 16), rows), :] = mine[...]
    out[pl.ds(pl.multiple_of((1 - core) * rows, 16), rows), :] = other[...]


def inner_back_kernel(flag, d_ffn, mine, other, slope_gate, slope_up, out, down):
    @pl.when(pl.program_id(0) == 0)
    def _():
        place_halves(flag, mine, other, down)

    width = down.shape[0]
    d_hidden = matmul_cols(d_ffn[...], down[...])
    out[:, :width] = (d_hidden * slope_gate[...]).astype(LOW)
    out[:, width:] = (d_hidden * slope_up[...]).astype(LOW)


def inner_back(flag, d_ffn, mine, other, slope_gate, slope_up, chips):
    rows, features = d_ffn.shape
    width = 2 * mine.shape[0]
    if width % LANES:
        d_hidden = matmul_cols(d_ffn, core_rows(mine, other))
        return jnp.concatenate([d_hidden * slope_gate, d_hidden * slope_up], axis=1).astype(LOW)
    tall = rows // chips
    flat = pl.BlockSpec((tall, width), lambda i: (i, 0))
    return pl.pallas_call(
        inner_back_kernel,
        grid=(chips,),
        in_specs=[
            SCALAR,
            pl.BlockSpec((tall, features), lambda i: (i, 0)),
            whole(mine.shape),
            whole(other.shape),
            flat,
            flat,
        ],
        out_specs=pl.BlockSpec((tall, 2 * width), lambda i: (i, 0)),
        out_shape=jax.ShapeDtypeStruct((rows, 2 * width), LOW),
        scratch_shapes=[pltpu.VMEM((width, features), LOW)],
        compiler_params=params(60),
        cost_estimate=FREE,
    )(flag, d_ffn, mine, other, slope_gate, slope_up)


def back_project_kernel(tiles, chips, d_out, mine, other, *refs):
    act, outs, total = (refs[0], refs[1:-1], refs[-1]) if chips == 0 else (None, refs, None)
    step = pl.program_id(0)
    columns = d_out.shape[1]

    def work(weights):
        grad = matmul_cols(d_out[...], weights[:, :columns])
        if act is not None:
            total[...] = jnp.sum(grad * act[...].astype(F32), axis=0, keepdims=True)
        spread(grad.astype(LOW), outs)

    @pl.when(step < tiles)
    def _():
        work(mine)

    @pl.when(step >= tiles)
    def _():
        work(other)


def back_project(d_out, mine, other, chips, *act):
    rows, columns = d_out.shape
    half = mine.shape[0]
    tile = 2 * LANES
    tiles = half // tile
    shapes = spread_shapes(chips, rows, 2 * half)
    flat = pl.BlockSpec((rows, tile), lambda i: (0, i))
    outs = pl.pallas_call(
        functools.partial(back_project_kernel, tiles, 0 if act else 1),
        grid=(2 * tiles,),
        in_specs=[
            whole(d_out.shape),
            pl.BlockSpec((tile, mine.shape[1]), lambda i: (jnp.minimum(i, tiles - 1), 0)),
            pl.BlockSpec((tile, mine.shape[1]), lambda i: (jnp.maximum(i - tiles, 0), 0)),
        ]
        + [flat for _ in act],
        out_specs=[column_spec(shape, tile) for shape in shapes]
        + [pl.BlockSpec((1, tile), lambda i: (0, i)) for _ in act],
        out_shape=[jax.ShapeDtypeStruct(shape, LOW) for shape in shapes]
        + [jax.ShapeDtypeStruct((1, 2 * half), F32) for _ in act],
        compiler_params=params(40),
        cost_estimate=FREE,
    )(d_out, mine, other, *act)
    return (outs[:-1], outs[-1]) if act else outs


def turned_kernel(count, left, right, *refs):
    arrived, outs = refs[:count], refs[count:]
    total = matmul_rows(left[...], right[...])
    if arrived:
        total = total + arrived[0][...].astype(F32)
    spread(total.astype(LOW), outs)


def turned(left, part, right, *arrived, chips=1):
    rows, half = left.shape[0], left.shape[1] // CORES
    width = right.shape[1]
    tile = LANES if width % (2 * LANES) else 2 * LANES
    shapes = spread_shapes(chips, half, width)
    outs = pl.pallas_call(
        functools.partial(turned_kernel, len(arrived)),
        grid=(width // tile,),
        in_specs=[
            pl.BlockSpec((rows, half), lambda i: (0, part)),
            pl.BlockSpec((rows, tile), lambda i: (0, i)),
        ]
        + [pl.BlockSpec((half, tile), lambda i: (0, i)) for _ in arrived],
        out_specs=[column_spec(shape, tile) for shape in shapes],
        out_shape=[jax.ShapeDtypeStruct(shape, LOW) for shape in shapes],
        compiler_params=params(60 if width > half * 2 else 32),
        cost_estimate=FREE,
    )(left, right, *arrived)
    return outs[0] if chips == 1 else outs


def inner_out_kernel(flag, left, mine, other, *refs):
    outs, down = refs[:-1], refs[-1]
    step = pl.program_id(0)

    @pl.when(step == 0)
    def _():
        place_halves(flag, mine, other, down)

    spread_step(step, matmul(left[...], down[...]).astype(LOW), outs)


def inner_out(flag, hidden, mine, other, chips):
    rows, width = hidden.shape
    features = mine.shape[1]
    if width % LANES:
        return [matmul(hidden, core_rows(mine, other)).astype(LOW)]
    tall = rows // chips
    shapes = spread_shapes(chips, rows, features)
    flat = pl.BlockSpec((tall, features), lambda i: (i, 0))
    return pl.pallas_call(
        inner_out_kernel,
        grid=(chips,),
        in_specs=[
            SCALAR,
            pl.BlockSpec((tall, width), lambda i: (i, 0)),
            whole(mine.shape),
            whole(other.shape),
        ],
        out_specs=[flat] if len(shapes) == 1 else [whole(shape) for shape in shapes],
        out_shape=[jax.ShapeDtypeStruct(shape, LOW) for shape in shapes],
        scratch_shapes=[pltpu.VMEM((width, features), LOW)],
        compiler_params=params(36),
        cost_estimate=FREE,
    )(flag, hidden, mine, other)


def half_kernel(flag, left, right, *refs):
    arrived, out = refs[:-1], refs[-1]
    rows = out.shape[0]
    start = left.shape[1] - rows
    wide = -(-rows // LANES) * LANES
    second = flag[0] > 0
    first = pl.multiple_of(jnp.where(second, left.shape[1] - wide, 0), LANES)
    total = matmul_rows(left[:, pl.ds(first, wide)], right[...])
    total = jnp.where(second, total[wide - rows :], total[:rows])
    if arrived:
        total = total + arrived[0][...].astype(F32)
    out[...] = total.astype(LOW)


def half_product(flag, left, right, *arrived):
    rows, columns = left.shape
    width = right.shape[1]
    half = columns // 2
    if columns % LANES:
        total = matmul_rows(left, right)
        total = jnp.where(flag[0] > 0, total[half:], total[:half])
        return sum([part.astype(F32) for part in arrived], total).astype(LOW)
    tile = 2 * LANES
    return pl.pallas_call(
        half_kernel,
        grid=(width // tile,),
        in_specs=[SCALAR, whole(left.shape), pl.BlockSpec((rows, tile), lambda i: (0, i))]
        + [pl.BlockSpec((half, tile), lambda i: (0, i)) for _ in arrived],
        out_specs=pl.BlockSpec((half, tile), lambda i: (0, i)),
        out_shape=jax.ShapeDtypeStruct((half, width), LOW),
        compiler_params=params(60),
        cost_estimate=FREE,
    )(flag, left, right, *arrived)


def per_device(
    tokens,
    out_cotangent,
    group_ids,
    attn_gain,
    query_weight,
    key_weight,
    value_weight,
    out_weight,
    ffn_gain,
    gate_weight,
    up_weight,
    down_weight,
):
    tok_count, features = tokens.shape[1:]
    weight_rows, inner = gate_weight.shape
    chips = chip_count()
    chip, core = own_chip(), own_core()
    ids = lax.iota(jnp.int32, chips)
    head_width, inner_width = features // chips, inner // chips
    half = features // CORES
    flag = jnp.full((1,), core, jnp.int32)
    tokens, out_cotangent = tokens[0], out_cotangent[0]

    gains = jnp.concatenate(
        [
            jnp.broadcast_to(attn_gain[:, None], (weight_rows, LANES // 2)),
            jnp.broadcast_to(ffn_gain[:, None], (weight_rows, LANES // 2)),
        ],
        axis=1,
    )

    def for_chip(weight, k):
        width = weight.shape[1] // chips
        return lax.dynamic_slice_in_dim(weight, (chip ^ k) * width, width, axis=1)

    def rows_of_chips(weights, *others):
        parts = [jnp.concatenate([for_chip(w, k) for w in weights], axis=1) for k in range(chips)]
        parts = [jnp.concatenate([part] + list(others), axis=1) for part in parts]
        return jnp.stack(in_order(chips_scatter(parts)))

    group_span = GPS * lax.axis_size("batch")
    onehot = (group_ids[0, :, None] == jnp.arange(group_span, dtype=jnp.int32)[None, :]).astype(F32)
    group_total = seq_sum(jnp.sum(onehot, axis=0, keepdims=True))
    own_total = jnp.sum(onehot * group_total, axis=-1)[:, None]
    weighting = tok_count * lax.axis_size("seq") / (GPS * own_total)
    d_final = out_cotangent.astype(F32) * weighting

    out_mine = batch_gather(out_weight, 0)
    qkv_rows = rows_of_chips([query_weight, key_weight, value_weight], gains)
    qkv_mine = batch_gather(after(qkv_rows, out_mine), 1).reshape(half, -1)
    tokens_sent = after(tokens, qkv_rows, group_total)
    tokens_near = gather_near(tokens_sent)
    tokens_far = gather_far(tokens_near)
    gathered = gathered_rows(tokens_sent, tokens_near, tokens_far)
    ffn_sent = after(d_final.astype(LOW), *tokens_near, *tokens_far)
    ffn_near = gather_near(ffn_sent)
    gate_weight, up_weight = after((gate_weight, up_weight), gathered)
    inner_rows = rows_of_chips([gate_weight, up_weight])
    inner_mine = batch_gather(inner_rows, 1).reshape(half, -1)
    down_mine = batch_gather(after(down_weight, inner_rows), 0)

    ffn_far = gather_far(ffn_near)
    out_sent = after(out_mine, inner_rows)
    out_near = gather_near(out_sent)
    qkv_mine = after(qkv_mine, inner_rows, *ffn_near)
    qkv_other = swap_core(qkv_mine)
    out_far = gather_far(out_near)
    columns = 3 * head_width
    gain_one, gain_two = (
        jnp.concatenate([qkv_mine[:, place], qkv_other[:, place]]).astype(F32)[None]
        for place in (columns, columns + LANES // 2)
    )
    act_one, qkv = project(flag, gathered, gain_one, qkv_mine, qkv_other, columns, chips)
    qkv = qkv.reshape(chips, tok_count, columns)
    place = chip ^ ids
    tails = swap_core(qkv[:, tok_count - WINDOW :, head_width:])
    before = jnp.where(core > 0, ids, chip ^ jnp.maximum(place - 1, 0))
    follow = jnp.where(core > 0, chip ^ jnp.minimum(place + 1, chips - 1), ids)
    preceded = ((core > 0) | (place > 0)).astype(jnp.int32)
    followed = (core == 0) | (place < chips - 1)
    rims = jnp.take(after(tails, *out_near), before, axis=0)
    mixed = attention(flag, preceded, qkv, rims)

    mixed = after(mixed, *out_far, *ffn_far)
    mixed_own = chips_scatter([mixed[k] for k in range(chips)])
    cell = head_width // CORES
    mixed_own = jnp.concatenate(
        [block[:, i * cell : (i + 1) * cell] for i in range(CORES) for block in mixed_own], axis=1
    )
    out_near = after(out_near, mixed)
    out_half = gathered_rows(out_sent, out_near, out_far)
    out_other = swap_core(out_half)
    resid, act_two_own = out_project(
        flag, mixed_own, out_half, out_other, tokens, gain_two, chips
    )

    d_ffn = gathered_rows(ffn_sent, ffn_near, ffn_far)
    act_two_own = after(act_two_own, d_ffn)
    act_near = gather_near(act_two_own)
    act_far = gather_far(after(act_near, inner_mine))
    act_two = gathered_rows(act_two_own, act_near, act_far)
    inner_mine = after(inner_mine, *act_near)
    inner_other = swap_core(inner_mine)
    first = inner_first(act_two, inner_mine)
    hidden, slope_gate, slope_up = inner_second(act_two, inner_other, first)
    down_send = half_product(1 - flag, hidden, d_ffn)
    down_back = swap_core(down_send)
    down_mine = after(down_mine, down_send)
    down_sum = half_product(flag, hidden, after(d_ffn, down_send, down_mine), down_back)
    down_other = swap_core(down_mine)
    down_grad = batch_scatter(down_sum, 0)
    d_gate_up = inner_back(
        flag, after(d_ffn, down_sum), down_mine, down_other, slope_gate, slope_up, chips
    )
    inner_send = matmul_rows(act_two[:, half:], d_gate_up).astype(LOW)
    act_parts = back_project(after(d_gate_up, inner_send), inner_mine, inner_other, chips)
    act_near = chips_sum_near(act_parts)
    inner_sum = turned(
        act_two, 0, after(d_gate_up, act_parts[0], down_grad), swap_core(inner_send)
    )
    act_far = chips_sum_far(act_parts, act_near)
    inner_sum = after(inner_sum, *act_near)
    inner_grad = batch_scatter(inner_sum.reshape(chips, half // chips, -1), 1)
    d_resid, d_attn, d_mixed_own, gain_two_part = middle(
        flag,
        *summands(act_parts, act_near, act_far),
        resid,
        gain_two,
        d_final,
        out_half,
        out_other,
        chips,
    )

    d_mixed_parts = chips_scatter([d_mixed_own[k] for k in range(chips)])
    d_mixed = jnp.stack(d_mixed_parts)
    d_qkv, lent = attention_back(flag, preceded, qkv, rims, d_mixed)
    lent = swap_core(lent)
    out_send = turned(mixed_own, 1, after(d_attn, d_qkv))
    out_back = swap_core(out_send)
    block_parts = inner_out(flag, after(hidden, d_mixed_own), down_mine, down_other, chips)
    block_near = chips_sum_near(block_parts)

    returned = jnp.where(followed[:, None, None], jnp.take(lent, follow, axis=0), 0)
    d_qkv = d_qkv.at[:, tok_count - WINDOW :, head_width:].add(returned)
    d_qkv = after(d_qkv.reshape(chips * tok_count, columns), *block_near)
    qkv_send = turned(act_one, 1, d_qkv)
    between = chips_sum_between(block_parts, after(block_near, qkv_send))
    block_far = chips_sum_send(between)
    qkv_sum = turned(act_one, 0, after(d_qkv, qkv_send, *between), swap_core(qkv_send))
    d_act_parts, gain_one_part = back_project(
        after(d_qkv, qkv_sum), qkv_mine, qkv_other, chips, act_one
    )
    qkv_sum = after(qkv_sum, inner_grad, d_act_parts[0])
    qkv_grad = batch_scatter(qkv_sum.reshape(chips, half // chips, -1), 1)

    out_parts = turned(mixed_own, 0, after(d_attn, d_act_parts[0]), out_back, chips=chips)
    out_parts = out_parts if chips > 1 else [out_parts]
    out_near = chips_sum_near(out_parts)
    gain_parts = jnp.concatenate([gain_one_part / gain_one, gain_two_part], axis=0)
    gain_core = swap_core(gain_parts[:, half:])
    d_act_parts = after(d_act_parts, *out_near)
    d_act_near = chips_sum_near(d_act_parts)
    out_far = chips_sum_far(out_parts, out_near)
    out_sum = summed(out_parts, out_near, out_far).astype(LOW)
    out_grad = batch_scatter(after(out_sum, qkv_grad), 0)

    def columns_of_chips(grad):
        chip_rows = [
            lax.dynamic_index_in_dim(grad, chip ^ k, axis=0, keepdims=False) for k in range(chips)
        ]
        return chips_scatter(chip_rows)

    inner_cells = columns_of_chips(after(inner_grad, qkv_grad))
    d_act_near = after(d_act_near, qkv_grad, *out_far)
    d_act_far = chips_sum_far(d_act_parts, d_act_near)
    qkv_cells = columns_of_chips(after(qkv_grad, *d_act_far))
    gain_grads = (gain_parts[:, :half] + after(gain_core, *out_near)).reshape(2, chips, -1)
    gain_grads = chips_scatter(
        [
            lax.dynamic_index_in_dim(gain_grads, chip ^ k, axis=1, keepdims=False)
            for k in range(chips)
        ]
    )
    row = lax.axis_index("batch")
    gain_grads = sum(gain_grads).reshape(2, lax.axis_size("batch"), -1)
    gain_grads = sum(
        exchange(
            lax.dynamic_index_in_dim(gain_grads, row ^ k, axis=1, keepdims=False), k, "batch"
        )
        for k in range(lax.axis_size("batch"))
    )
    tokens_grad = last(
        flag, *summands(d_act_parts, d_act_near, d_act_far), tokens, gain_one, d_resid, chips
    )
    block_out = (resid + summed(block_parts, block_near, block_far)).astype(LOW)

    inner_grad, qkv_grad = in_order(inner_cells), in_order(qkv_cells)

    def whole_columns(blocks, first, width):
        parts = [block[:, first : first + width] for block in blocks]
        return jnp.concatenate(parts, axis=1).astype(F32)


    return (
        block_out[None],
        tokens_grad[None],
        gain_grads[0],
        whole_columns(qkv_grad, 0, head_width),
        whole_columns(qkv_grad, head_width, head_width),
        whole_columns(qkv_grad, 2 * head_width, head_width),
        out_grad.astype(F32),
        gain_grads[1],
        whole_columns(inner_grad, 0, inner_width),
        whole_columns(inner_grad, inner_width, inner_width),
        down_grad.astype(F32),
    )


def solution(mesh):
    rows = P(("seq", "batch"), None)
    vector = P(("seq", "batch"))
    cells = P("batch", "seq", None)
    return jax.shard_map(
        per_device,
        mesh=mesh,
        in_specs=(cells, cells, P("batch", "seq"))
        + (vector, rows, rows, rows, rows, vector, rows, rows, rows),
        out_specs=(cells, cells, vector, rows, rows, rows, rows, vector, rows, rows, rows),
        check_vma=False,
    )
```
